32 devices in a mesh: groups: 2 (over x), seq: 8 (over z, y), head: 2 (over core).
Axes of the slice: x: 2, y: 2, z: 4, core: 2. Of those that a mesh axis runs over, the one named last changes fastest.
Arguments:
- queries: bfloat16 [2, 3072, 2048], P(None, ('groups', 'seq'), 'head'), parts along dimension 1, may hold values from -6 to 6
- keys: bfloat16 [2, 3072, 2048], P(None, ('groups', 'seq'), 'head'), parts along dimension 1, may hold values from -6 to 6
- values: bfloat16 [2, 3072, 2048], P(None, ('groups', 'seq'), 'head'), parts along dimension 1, may hold values from -6 to 6
- rates: float32 [2, 3072, 4], P(None, ('groups', 'seq'), 'head'), parts along dimension 1, may hold values from 0.0005638186 to 0.0056381864
- fast_init: bfloat16 [3, 4, 512, 512], P(None, 'head'), may hold values from -0.8838835 to 0.8838835
- out_proj: bfloat16 [2048, 2048], P('seq'), may hold values from -0.125 to 0.125
Outputs:
- projected: bfloat16 [2, 3072, 2048], P(None, ('groups', 'seq', 'head')), parts along dimension 1
The draws below stay inside these ranges and needn't reach their ends.
There are 2 independent parts, one for each index of `groups`. The reference program is written for one: setup_inputs(seed, part) draws one part's arguments, and reference() takes and returns one part's arrays. A program takes and returns all parts, laid end to end along the dimension named above; an argument that names none is the same for every part. Nothing has to cross between parts.
All inputs are finite; a program needn't handle non-finite values.
Results may differ from the reference program's by a relative error of at most 0.012.
The reference program's roundings to bfloat16 on the way count: a program that leaves them out, or rounds other values in their place, can miss the bound.
Values may be sent and summed in bfloat16 or wider, within the bound.
No kernel may reach another device: no remote copies, remote signals or barrier semaphores. Data moves between devices by JAX's collectives and lax.ppermute only.
A program may use at most 128 MiB of HBM per device.

```python
import math
import jax
import jax.numpy as jnp
from jax import lax

HEADS = 4
HD = 512
D = 2048
BLOCKS = 2
TOKENS = 1536


def draw_fast_init(key, part):
    key_base, key_rows, key_cols = jax.random.split(key, 3)
    shape = (3, HEADS, HD, HD)
    base = jnp.clip(jax.random.normal(key_base, shape, jnp.float32), -4.0, 4.0)
    row_scale = jnp.exp(jax.random.uniform(key_rows, (3, HEADS, HD, 1), jnp.float32, math.log(0.3), math.log(3.0)))
    col_scale = jnp.exp(jax.random.uniform(key_cols, (3, HEADS, 1, HD), jnp.float32, math.log(0.7), math.log(1.4)))
    return (base * row_scale * col_scale * (1.0 / math.sqrt(HD))).astype(jnp.bfloat16)


def level_of(rng, extent, cuts, least, high):
    def one(position, shards_of):
        steps = jax.random.uniform(jax.random.fold_in(jax.random.fold_in(rng, 6), position), (shards_of,), jnp.float32, least / len(cuts), high / len(cuts))
        return jnp.repeat(jnp.exp(steps), extent[position] // shards_of).reshape((-1,) + (1,) * (len(extent) - position - 1))

    factor_of = one(*cuts[0])
    for cut in cuts[1:]:
        factor_of = factor_of * one(*cut)
    return factor_of


def noise(rng, shape, deviation, bound, cuts=(), held_as=jnp.bfloat16):
    level = level_of(rng, shape, cuts, -0.22, 0.18) if cuts else 1.0
    values = jax.random.normal(rng, shape, jnp.float32) * deviation * level
    return jnp.minimum(jnp.maximum(values, -bound), bound).astype(held_as)


def setup_inputs(seed: int = 0, part: int = 0) -> dict:
    arg_keys = jax.random.split(jax.random.key(seed), 7)
    part_keys = jax.random.split(jax.random.fold_in(arg_keys[6], part), 7)
    queries = noise(part_keys[0], (BLOCKS, TOKENS, D), 1.0, 6.0, ((1, 8), (2, 2)))
    keys = noise(part_keys[1], (BLOCKS, TOKENS, D), 1.0, 6.0, ((1, 8), (2, 2)))
    values = noise(part_keys[2], (BLOCKS, TOKENS, D), 1.0, 6.0, ((1, 8), (2, 2)))
    rates = jnp.clip(jnp.exp(math.log(0.0056381864) - 2.3025851 * jax.random.uniform(part_keys[3], (BLOCKS, TOKENS, HEADS), jnp.float32) ** level_of(part_keys[3], (BLOCKS, TOKENS, HEADS), ((1, 8), (2, 2)), -0.2, 0.2)), 0.0005638186, 0.0056381864)
    fast_init = draw_fast_init(jax.random.fold_in(arg_keys[6], 71), part)
    out_proj = noise(arg_keys[5], (D, D), D ** -0.5, 0.125, ((0, 8),))
    return {"queries": queries, "keys": keys, "values": values, "rates": rates, "fast_init": fast_init, "out_proj": out_proj}


def silu_parts(value):
    sigma = jax.nn.sigmoid(value)
    return (value * sigma, sigma * (1.0 + value * (1.0 - sigma)))

def head_update(weights, keys_head, values_head, rates_head):
    gate_pre = jnp.dot(keys_head, weights[0].T, preferred_element_type=jnp.float32)
    up_pre = jnp.dot(keys_head, weights[1].T, preferred_element_type=jnp.float32)
    gate_act, gate_slope = silu_parts(gate_pre)
    hidden = (gate_act * up_pre).astype(jnp.bfloat16)
    weighted = (rates_head[:, None] * values_head.astype(jnp.float32)).astype(jnp.bfloat16)
    back = jnp.dot(weighted, weights[2], preferred_element_type=jnp.float32)
    grad_gate = (back * up_pre * gate_slope).astype(jnp.bfloat16)
    grad_up = (back * gate_act).astype(jnp.bfloat16)
    update = jnp.stack([jnp.dot(grad_gate.T, keys_head, preferred_element_type=jnp.float32), jnp.dot(grad_up.T, keys_head, preferred_element_type=jnp.float32), jnp.dot(weighted.T, hidden, preferred_element_type=jnp.float32)])
    return weights.astype(jnp.float32) + update

def normalize(summed, target):
    scale = lax.rsqrt(lax.optimization_barrier(jnp.mean(summed * summed, axis=-1, keepdims=True)) + 1e-06)
    return (summed * target * scale).astype(jnp.bfloat16)

def apply_fast(weights, queries_head):
    gate_pre = jnp.dot(queries_head, weights[0].T, preferred_element_type=jnp.float32)
    up_pre = jnp.dot(queries_head, weights[1].T, preferred_element_type=jnp.float32)
    gate_act, gate_slope = silu_parts(gate_pre)
    applied = (gate_act * up_pre).astype(jnp.bfloat16)
    return jnp.dot(applied, weights[2].T, preferred_element_type=jnp.float32).astype(jnp.bfloat16)

def reference(queries, keys, values, rates, fast_init, out_proj):
    init_float = fast_init.astype(jnp.float32)
    target = jnp.sqrt(lax.optimization_barrier(jnp.mean(init_float * init_float, axis=-1, keepdims=True)))
    current = [fast_init[:, head_idx] for head_idx in range(HEADS)]
    results = []
    for block_idx in range(BLOCKS):
        pieces = []
        for head_idx in range(HEADS):
            first = head_idx * HD
            summed = head_update(current[head_idx], keys[block_idx][:, first:first + HD], values[block_idx][:, first:first + HD], rates[block_idx][:, head_idx])
            current[head_idx] = normalize(summed, target[:, head_idx])
            pieces.append(apply_fast(current[head_idx], queries[block_idx][:, first:first + HD]))
        mixed = jnp.concatenate(pieces, axis=1)
        results.append(jnp.dot(mixed, out_proj, preferred_element_type=jnp.float32).astype(jnp.bfloat16))
    return jnp.stack(results)
```

```python
import functools

import jax
import jax.numpy as jnp
from jax import lax
from jax.experimental import pallas as pl
from jax.experimental.pallas import tpu as pltpu
from jax.sharding import PartitionSpec as P

VMEM_LIMIT = 40 * 1024 * 1024
BOTH = ("seq", "head")


def silu_parts(value):
    sigma = jax.nn.sigmoid(value)
    return (value * sigma, sigma * (1.0 + value * (1.0 - sigma)))


def dot(left, right, left_dim, right_dim):
    return lax.dot_general(
        left, right, (((left_dim,), (right_dim,)), ((), ())), preferred_element_type=jnp.float32
    )


def local_update(weights, keys_local, values_local, rates_local):
    gate_pre = jnp.einsum(
        "thi,hoi->tho", keys_local, weights[0], preferred_element_type=jnp.float32
    )
    up_pre = jnp.einsum("thi,hoi->tho", keys_local, weights[1], preferred_element_type=jnp.float32)
    gate_act, gate_slope = silu_parts(gate_pre)
    hidden = (gate_act * up_pre).astype(jnp.bfloat16)
    weighted = (rates_local[:, :, None] * values_local.astype(jnp.float32)).astype(jnp.bfloat16)
    back = jnp.einsum("tho,hog->thg", weighted, weights[2], preferred_element_type=jnp.float32)
    grad_gate = (back * up_pre * gate_slope).astype(jnp.bfloat16)
    grad_up = (back * gate_act).astype(jnp.bfloat16)
    return jnp.stack(
        [
            jnp.einsum("thg,thi->hgi", grad_gate, keys_local, preferred_element_type=jnp.float32),
            jnp.einsum("thg,thi->hgi", grad_up, keys_local, preferred_element_type=jnp.float32),
            jnp.einsum("tho,thg->hog", weighted, hidden, preferred_element_type=jnp.float32),
        ]
    )


def apply_local(weights, queries_local):
    gate_pre = jnp.einsum(
        "thi,hoi->tho", queries_local, weights[0], preferred_element_type=jnp.float32
    )
    up_pre = jnp.einsum(
        "thi,hoi->tho", queries_local, weights[1], preferred_element_type=jnp.float32
    )
    gate_act, gate_slope = silu_parts(gate_pre)
    applied = (gate_act * up_pre).astype(jnp.bfloat16)
    produced = jnp.einsum("thg,hog->tho", applied, weights[2], preferred_element_type=jnp.float32)
    return produced.astype(jnp.bfloat16).reshape(queries_local.shape[0], -1)


def local_summed(queries, keys, values, rates, fast_init, out_proj):
    block_count, tok_count, width_here = queries.shape
    heads_here = fast_init.shape[1]
    head_width = fast_init.shape[2]
    init_float = fast_init.astype(jnp.float32)
    target = jnp.sqrt(jnp.mean(init_float * init_float, axis=-1, keepdims=True))
    row_count = head_width // lax.axis_size("seq")
    offset = lax.axis_index("seq") * row_count
    current = fast_init
    produced_list = []
    for block_idx in range(block_count):
        keys_local = keys[block_idx].reshape(tok_count, heads_here, head_width)
        values_local = values[block_idx].reshape(tok_count, heads_here, head_width)
        update = local_update(current, keys_local, values_local, rates[block_idx])
        shard = lax.psum_scatter(update, "seq", scatter_dimension=3, tiled=True)
        own = lax.dynamic_slice_in_dim(current, offset, row_count, 3).astype(jnp.float32) + shard
        squares = lax.psum(jnp.sum(own * own, axis=-1, keepdims=True), "seq")
        fresh = (own * target * lax.rsqrt(squares / head_width + 1e-06)).astype(jnp.bfloat16)
        current = lax.all_gather(fresh, "seq", axis=3, tiled=True)
        produced = apply_local(
            current, queries[block_idx].reshape(tok_count, heads_here, head_width)
        )
        produced_list.append(produced)
    mixed = lax.all_to_all(
        jnp.stack(produced_list), "head", split_axis=1, concat_axis=2, tiled=True
    )
    result = jnp.einsum(
        "ctf,fd->ctd",
        mixed,
        lax.all_gather(out_proj, "seq", axis=0, tiled=True),
        preferred_element_type=jnp.float32,
    )
    return result.astype(jnp.bfloat16)


def pack_kernel(place, keys, values, rates, *messages):
    half, width = messages[0].shape[1:]
    row = place[0]
    for turn, message in enumerate(messages):
        want = row ^ turn
        head_bit, half_bit = want >> 1, want & 1
        rows = pl.ds(pl.multiple_of(half_bit * half, half), half)
        cols = pl.ds(pl.multiple_of(head_bit * width, width), width)
        message[0] = keys[0, rows, cols]
        rate = rates[0, rows, :]
        rate = jnp.where(head_bit == 0, rate[:, 0:1], rate[:, 1:2])
        message[1] = (rate * values[0, rows, cols].astype(jnp.float32)).astype(jnp.bfloat16)


def pack_queries_kernel(place, queries, *messages):
    half, width = messages[0].shape[1:]
    row = place[0]
    for turn, message in enumerate(messages):
        want = row ^ turn
        head_bit, half_bit = want >> 1, want & 1
        rows = pl.ds(pl.multiple_of(half_bit * half, half), half)
        cols = pl.ds(pl.multiple_of(head_bit * width, width), width)
        for block in range(queries.shape[0]):
            message[block] = queries[block, rows, cols]


def pack(place, block, keys, values, rates):
    tokens, both = keys.shape[1:]
    shape = (2, tokens // 2, both // 2)
    one = lambda arr: pl.BlockSpec((1,) + arr.shape[1:], lambda i, p: (block, 0, 0))
    whole = pl.BlockSpec(shape, lambda i, p: (0, 0, 0))
    return pl.pallas_call(
        pack_kernel,
        grid_spec=pltpu.PrefetchScalarGridSpec(
            num_scalar_prefetch=1,
            grid=(1,),
            in_specs=[one(keys), one(values), one(rates)],
            out_specs=[whole] * 4,
        ),
        out_shape=[jax.ShapeDtypeStruct(shape, jnp.bfloat16)] * 4,
        name="pack",
    )(place, keys, values, rates)


def pack_queries(place, queries):
    blocks, tokens, both = queries.shape
    shape = (blocks, tokens // 2, both // 2)
    whole = pl.BlockSpec(shape, lambda i, p: (0, 0, 0))
    return pl.pallas_call(
        pack_queries_kernel,
        grid_spec=pltpu.PrefetchScalarGridSpec(
            num_scalar_prefetch=1,
            grid=(1,),
            in_specs=[pl.BlockSpec(queries.shape, lambda i, p: (0, 0, 0))],
            out_specs=[whole] * 4,
        ),
        out_shape=[jax.ShapeDtypeStruct(shape, jnp.bfloat16)] * 4,
        name="pack_queries",
    )(place, queries)


def step_kernel(chunks, block, tile, place, *refs):
    pieces = refs[:chunks]
    asked = refs[chunks : chunks + 4]
    weights, target = refs[chunks + 4 : chunks + 6]
    fresh = refs[chunks + 6]
    produced = refs[chunks + 7 : chunks + 11]
    keys, values, hidden, grad_gate, grad_up, queries, sems = refs[chunks + 11 :]
    half = pieces[0].shape[1]
    copies = []
    for idx, piece in enumerate(pieces):
        rows = pl.ds(idx * half, half)
        copies.append(pltpu.make_async_copy(piece.at[0], keys.at[rows], sems.at[2 * idx]))
        copies.append(pltpu.make_async_copy(piece.at[1], values.at[rows], sems.at[2 * idx + 1]))
    row, core = place[0], place[2]
    shift = row ^ (2 * (row & 1) + core)
    for turn, ask in enumerate(asked):
        rows = pl.ds(pl.multiple_of((shift ^ turn) * half, half), half)
        copies.append(
            pltpu.make_async_copy(ask.at[block], queries.at[rows], sems.at[2 * chunks + turn])
        )
    for copy in copies:
        copy.start()
    for copy in copies:
        copy.wait()

    total = keys.shape[0]
    for start in range(0, total, tile):
        rows = pl.ds(start, tile)
        key, value = keys[rows], values[rows]
        gate_pre = dot(key, weights[0], 1, 1)
        up_pre = dot(key, weights[1], 1, 1)
        back = dot(value, weights[2], 1, 0)
        gate_act, gate_slope = silu_parts(gate_pre)
        hidden[rows] = (gate_act * up_pre).astype(jnp.bfloat16)
        grad_gate[rows] = (back * up_pre * gate_slope).astype(jnp.bfloat16)
        grad_up[rows] = (back * gate_act).astype(jnp.bfloat16)

    for idx, (left, right) in enumerate(((grad_gate, keys), (grad_up, keys), (values, hidden))):
        summed = weights[idx].astype(jnp.float32) + dot(left[...], right[...], 0, 0)
        mean = jnp.mean(summed * summed, axis=-1, keepdims=True)
        fresh[idx] = (summed * target[idx] * lax.rsqrt(mean + 1e-06)).astype(jnp.bfloat16)

    query = queries[...]
    gate_pre = dot(query, fresh[0], 1, 1)
    up_pre = dot(query, fresh[1], 1, 1)
    applied = (gate_pre * jax.nn.sigmoid(gate_pre) * up_pre).astype(jnp.bfloat16)
    out = dot(applied, fresh[2], 1, 1).astype(jnp.bfloat16)
    for idx, ref in enumerate(produced):
        ref[...] = out[idx * half : (idx + 1) * half]


def step(place, block, pieces, asked, weights, target):
    half, width = pieces[0].shape[1:]
    total = half * len(pieces)
    tile = 256 if total % 256 == 0 else half
    vmem = pl.BlockSpec(memory_space=pltpu.VMEM)
    anywhere = pl.BlockSpec(memory_space=pl.ANY)
    token_buf = pltpu.VMEM((total, width), jnp.bfloat16)
    flops = 2 * width * width * (6 * total + 12 * half)
    outs = pl.pallas_call(
        functools.partial(step_kernel, len(pieces), block, tile),
        in_specs=[pl.BlockSpec(memory_space=pltpu.SMEM)]
        + [anywhere] * (len(pieces) + 4)
        + [vmem, vmem],
        out_specs=[vmem] * 5,
        out_shape=[jax.ShapeDtypeStruct(weights.shape, jnp.bfloat16)]
        + [jax.ShapeDtypeStruct((half, width), jnp.bfloat16)] * 4,
        scratch_shapes=[token_buf] * 5
        + [
            pltpu.VMEM((4 * half, width), jnp.bfloat16),
            pltpu.SemaphoreType.DMA((2 * len(pieces) + 4,)),
        ],
        compiler_params=pltpu.CompilerParams(vmem_limit_bytes=VMEM_LIMIT),
        cost_estimate=pl.CostEstimate(
            flops=flops, bytes_accessed=8 * 1024 * 1024, transcendentals=total * width
        ),
        name="step",
    )(place, *pieces, *asked, weights, target)
    return outs[0], outs[1:]


def project_kernel(blocks, place, *refs):
    slabs = refs[:8]
    mixed = refs[8 : 8 + 4 * blocks]
    out, matrix, sems = refs[8 + 4 * blocks :]
    part = slabs[0].shape[1]
    line, core, group = place[1], place[2], place[3]
    copies = []
    for idx, slab in enumerate(slabs):
        here_line = line ^ (idx & 1)
        here_group = group ^ ((idx >> 1) & 1)
        here_core = core ^ (idx >> 2)
        at = (here_line * 4 + here_group * 2 + here_core) * part
        rows = pl.ds(pl.multiple_of(at, part), part)
        copies.append(pltpu.make_async_copy(slab, matrix.at[:, rows], sems.at[idx]))
    for copy in copies:
        copy.start()
    for copy in copies:
        copy.wait()
    for block in range(blocks):
        total = None
        for turn in range(4):
            term = dot(mixed[4 * block + turn][...], matrix[turn], 1, 0)
            total = term if total is None else total + term
        out[block] = total.astype(jnp.bfloat16)


def project(place, slabs, mixed):
    blocks = len(mixed) // 4
    half, width = mixed[0].shape
    depth = slabs[0].shape[2]
    vmem = pl.BlockSpec(memory_space=pltpu.VMEM)
    anywhere = pl.BlockSpec(memory_space=pl.ANY)
    return pl.pallas_call(
        functools.partial(project_kernel, blocks),
        in_specs=[pl.BlockSpec(memory_space=pltpu.SMEM)] + [anywhere] * 8 + [vmem] * len(mixed),
        out_specs=vmem,
        out_shape=jax.ShapeDtypeStruct((blocks, half, depth), jnp.bfloat16),
        scratch_shapes=[
            pltpu.VMEM((4, width, depth), jnp.bfloat16),
            pltpu.SemaphoreType.DMA((8,)),
        ],
        compiler_params=pltpu.CompilerParams(vmem_limit_bytes=VMEM_LIMIT),
        cost_estimate=pl.CostEstimate(
            flops=2 * blocks * half * 4 * width * depth,
            bytes_accessed=10 * 1024 * 1024,
            transcendentals=0,
        ),
        name="project",
    )(place, *slabs, *mixed)


def routes(rule):
    pairs = []
    for row in range(4):
        for line in range(2):
            for core in range(2):
                to_row, to_line, to_core = rule(row, line, core)
                pairs.append(((row * 2 + line) * 2 + core, (to_row * 2 + to_line) * 2 + to_core))
    return pairs


def spread_rule(turn):
    def rule(row, line, core):
        want = row ^ turn
        return (2 * core + (want >> 1), line, want & 1)

    return rule


def swap_line(arr):
    return lax.ppermute(arr, BOTH, routes(lambda row, line, core: (row, 1 - line, core)))


def swap_core(arr):
    return lax.ppermute(arr, BOTH, routes(lambda row, line, core: (row, line, 1 - core)))


def swap_row(arr, turn):
    return lax.ppermute(arr, BOTH, routes(lambda row, line, core: (row ^ turn, line, core)))


def swap_group(arr):
    return lax.ppermute(arr, "groups", [(0, 1), (1, 0)])


def spread(messages):
    return [
        lax.ppermute(message, BOTH, routes(spread_rule(turn)))
        for turn, message in enumerate(messages)
    ]


def local_gathered(queries, keys, values, rates, fast_init, out_proj):
    block_count = queries.shape[0]
    seq, core, group = lax.axis_index("seq"), lax.axis_index("head"), lax.axis_index("groups")
    row, line = seq // 2, seq % 2
    place = jnp.stack([row, line, core, group]).astype(jnp.int32)

    pieces = []
    for block in range(block_count):
        own = spread(pack(place, block, keys, values, rates))
        lines = own + [swap_line(arr) for arr in own]
        pieces.append(lines + [swap_core(arr) for arr in lines])
    asked = spread(pack_queries(place, queries))

    mine = lax.dynamic_index_in_dim(fast_init, row % 2, 1, keepdims=False)
    weights = jnp.where(core == row // 2, mine, swap_core(mine))
    init_float = weights.astype(jnp.float32)
    target = jnp.sqrt(jnp.mean(init_float * init_float, axis=-1, keepdims=True))

    part = out_proj.shape[0] // 4
    quarter = lax.dynamic_slice_in_dim(out_proj, (2 * group + core) * part, part, 0)
    slab = jnp.stack([quarter] + [swap_row(quarter, turn) for turn in (1, 2, 3)])
    slab_line = swap_line(slab)
    slabs = [slab, slab_line, swap_group(slab), swap_group(slab_line)]
    slabs = slabs + [swap_core(arr) for arr in slabs]

    mixed = []
    for block in range(block_count):
        weights, produced = step(place, block, pieces[block], asked, weights, target)
        mixed += [produced[0]] + [swap_row(produced[turn], turn) for turn in (1, 2, 3)]
    return project(place, slabs, mixed)


def solution(mesh):
    in_specs = (
        P(None, ("groups", "seq"), "head"),
        P(None, ("groups", "seq"), "head"),
        P(None, ("groups", "seq"), "head"),
        P(None, ("groups", "seq"), "head"),
        P(None, "head", None, None),
        P("seq", None),
    )
    out_specs = P(None, ("groups", "seq", "head"), None)
    few = dict(mesh.shape) == {"groups": 2, "seq": 8, "head": 2}
    local = local_gathered if few else local_summed
    return jax.shard_map(local, mesh=mesh, in_specs=in_specs, out_specs=out_specs, check_vma=False)
```

```python
import functools

import jax
import jax.numpy as jnp
from jax import lax
from jax.experimental import pallas as pl
from jax.experimental.pallas import tpu as pltpu
from jax.sharding import PartitionSpec as P

VMEM_LIMIT = 40 * 1024 * 1024
BOTH = ("seq", "head")


def silu_parts(value):
    sigma = jax.nn.sigmoid(value)
    return (value * sigma, sigma * (1.0 + value * (1.0 - sigma)))


def dot(left, right, left_dim, right_dim):
    return lax.dot_general(
        left, right, (((left_dim,), (right_dim,)), ((), ())), preferred_element_type=jnp.float32
    )


def local_update(weights, keys_local, values_local, rates_local):
    gate_pre = jnp.einsum(
        "thi,hoi->tho", keys_local, weights[0], preferred_element_type=jnp.float32
    )
    up_pre = jnp.einsum("thi,hoi->tho", keys_local, weights[1], preferred_element_type=jnp.float32)
    gate_act, gate_slope = silu_parts(gate_pre)
    hidden = (gate_act * up_pre).astype(jnp.bfloat16)
    weighted = (rates_local[:, :, None] * values_local.astype(jnp.float32)).astype(jnp.bfloat16)
    back = jnp.einsum("tho,hog->thg", weighted, weights[2], preferred_element_type=jnp.float32)
    grad_gate = (back * up_pre * gate_slope).astype(jnp.bfloat16)
    grad_up = (back * gate_act).astype(jnp.bfloat16)
    return jnp.stack(
        [
            jnp.einsum("thg,thi->hgi", grad_gate, keys_local, preferred_element_type=jnp.float32),
            jnp.einsum("thg,thi->hgi", grad_up, keys_local, preferred_element_type=jnp.float32),
            jnp.einsum("tho,thg->hog", weighted, hidden, preferred_element_type=jnp.float32),
        ]
    )


def apply_local(weights, queries_local):
    gate_pre = jnp.einsum(
        "thi,hoi->tho", queries_local, weights[0], preferred_element_type=jnp.float32
    )
    up_pre = jnp.einsum(
        "thi,hoi->tho", queries_local, weights[1], preferred_element_type=jnp.float32
    )
    gate_act, gate_slope = silu_parts(gate_pre)
    applied = (gate_act * up_pre).astype(jnp.bfloat16)
    produced = jnp.einsum("thg,hog->tho", applied, weights[2], preferred_element_type=jnp.float32)
    return produced.astype(jnp.bfloat16).reshape(queries_local.shape[0], -1)


def local_summed(queries, keys, values, rates, fast_init, out_proj):
    block_count, tok_count, width_here = queries.shape
    heads_here = fast_init.shape[1]
    head_width = fast_init.shape[2]
    init_float = fast_init.astype(jnp.float32)
    target = jnp.sqrt(jnp.mean(init_float * init_float, axis=-1, keepdims=True))
    row_count = head_width // lax.axis_size("seq")
    offset = lax.axis_index("seq") * row_count
    current = fast_init
    produced_list = []
    for block_idx in range(block_count):
        keys_local = keys[block_idx].reshape(tok_count, heads_here, head_width)
        values_local = values[block_idx].reshape(tok_count, heads_here, head_width)
        update = local_update(current, keys_local, values_local, rates[block_idx])
        shard = lax.psum_scatter(update, "seq", scatter_dimension=3, tiled=True)
        own = lax.dynamic_slice_in_dim(current, offset, row_count, 3).astype(jnp.float32) + shard
        squares = lax.psum(jnp.sum(own * own, axis=-1, keepdims=True), "seq")
        fresh = (own * target * lax.rsqrt(squares / head_width + 1e-06)).astype(jnp.bfloat16)
        current = lax.all_gather(fresh, "seq", axis=3, tiled=True)
        produced = apply_local(
            current, queries[block_idx].reshape(tok_count, heads_here, head_width)
        )
        produced_list.append(produced)
    mixed = lax.all_to_all(
        jnp.stack(produced_list), "head", split_axis=1, concat_axis=2, tiled=True
    )
    result = jnp.einsum(
        "ctf,fd->ctd",
        mixed,
        lax.all_gather(out_proj, "seq", axis=0, tiled=True),
        preferred_element_type=jnp.float32,
    )
    return result.astype(jnp.bfloat16)


def pack_kernel(place, queries, keys, values, rates, *refs):
    packed, asked = refs[:8], refs[8:12]
    keys_in, values_in, queries_in, load_sems, sems = refs[12:]
    half, width = asked[0].shape[1:]
    row = place[0]
    blocks = keys_in.shape[0]
    loads = []
    for block in range(blocks):
        for source, target in ((keys, keys_in), (values, values_in), (queries, queries_in)):
            sem = load_sems.at[len(loads)]
            loads.append(pltpu.make_async_copy(source.at[block], target.at[block], sem))
            loads[-1].start()
    spots = []
    for turn in range(4):
        want = row ^ turn
        rows = pl.ds(pl.multiple_of((want & 1) * half, half), half)
        cols = pl.ds(pl.multiple_of((want >> 1) * width, width), width)
        spots.append((rows, cols))
    copies = []

    def send(source, target):
        copies.append(pltpu.make_async_copy(source, target, sems.at[len(copies)]))
        copies[-1].start()

    for block in range(blocks):
        loads[3 * block].wait()
        for turn, (rows, cols) in enumerate(spots):
            send(keys_in.at[block, rows, cols], packed[4 * block + turn].at[0])
        loads[3 * block + 1].wait()
        rate = rates[block].T
        for head in range(2):
            cols = slice(head * width, (head + 1) * width)
            scaled = rate[:, head : head + 1] * values_in[block, :, cols].astype(jnp.float32)
            values_in[block, :, cols] = scaled.astype(jnp.bfloat16)
        for turn, (rows, cols) in enumerate(spots):
            send(values_in.at[block, rows, cols], packed[4 * block + turn].at[1])
    for block in range(blocks):
        loads[3 * block + 2].wait()
        for turn, (rows, cols) in enumerate(spots):
            send(queries_in.at[block, rows, cols], asked[turn].at[block])
    for copy in copies:
        copy.wait()


def pack(place, queries, keys, values, rates):
    blocks, tokens, both = keys.shape
    half, width = tokens // 2, both // 2
    vmem = pl.BlockSpec(memory_space=pltpu.VMEM)
    hbm = pl.BlockSpec(memory_space=pltpu.HBM)
    anywhere = pl.BlockSpec(memory_space=pl.ANY)
    outs = pl.pallas_call(
        pack_kernel,
        in_specs=[pl.BlockSpec(memory_space=pltpu.SMEM), hbm, hbm, hbm, vmem],
        out_specs=[anywhere] * 12,
        out_shape=[jax.ShapeDtypeStruct((2, half, width), jnp.bfloat16)] * 8
        + [jax.ShapeDtypeStruct((blocks, half, width), jnp.bfloat16)] * 4,
        scratch_shapes=[
            pltpu.VMEM(keys.shape, jnp.bfloat16),
            pltpu.VMEM(keys.shape, jnp.bfloat16),
            pltpu.VMEM(keys.shape, jnp.bfloat16),
            pltpu.SemaphoreType.DMA((3 * blocks,)),
            pltpu.SemaphoreType.DMA((12 * blocks,)),
        ],
        name="pack",
    )(place, queries, keys, values, rates)
    return outs[:4], outs[4:8], outs[8:]


def collect_kernel(*refs):
    rounds, out = refs[:4], refs[4]
    half = rounds[0].shape[1]
    for idx, message in enumerate(rounds):
        out[:, idx * half : (idx + 1) * half] = message[...]


def collect(rounds):
    kinds, half, width = rounds[0].shape
    vmem = pl.BlockSpec(memory_space=pltpu.VMEM)
    return pl.pallas_call(
        collect_kernel,
        in_specs=[vmem] * 4,
        out_specs=vmem,
        out_shape=jax.ShapeDtypeStruct((kinds, 4 * half, width), jnp.bfloat16),
        name="collect",
    )(*rounds)


def step_kernel(chunks, block, tile, place, *refs):
    pieces = refs[:chunks]
    asked = refs[chunks : chunks + 4]
    weights, target = refs[chunks + 4 : chunks + 6]
    fresh = refs[chunks + 6]
    produced = refs[chunks + 7 : chunks + 11]
    keys, values, hidden, grad_gate, grad_up, queries, sems = refs[chunks + 11 :]
    size, half = pieces[0].shape[1], produced[0].shape[0]
    copies = []
    for idx, piece in enumerate(pieces):
        rows = pl.ds(idx * size, size)
        copies.append(pltpu.make_async_copy(piece.at[0], keys.at[rows], sems.at[2 * idx]))
        copies.append(pltpu.make_async_copy(piece.at[1], values.at[rows], sems.at[2 * idx + 1]))
    row, core = place[0], place[2]
    shift = row ^ (2 * (row & 1) + core)
    for turn, ask in enumerate(asked):
        rows = pl.ds(pl.multiple_of((shift ^ turn) * half, half), half)
        copies.append(
            pltpu.make_async_copy(ask.at[block], queries.at[rows], sems.at[2 * chunks + turn])
        )
    for copy in copies:
        copy.start()
    for copy in copies:
        copy.wait()

    total = keys.shape[0]
    for start in range(0, total, tile):
        rows = pl.ds(start, tile)
        key, value = keys[rows], values[rows]
        gate_pre = dot(key, weights[0], 1, 1)
        up_pre = dot(key, weights[1], 1, 1)
        back = dot(value, weights[2], 1, 0)
        gate_act, gate_slope = silu_parts(gate_pre)
        hidden[rows] = (gate_act * up_pre).astype(jnp.bfloat16)
        grad_gate[rows] = (back * up_pre * gate_slope).astype(jnp.bfloat16)
        grad_up[rows] = (back * gate_act).astype(jnp.bfloat16)

    for idx, (left, right) in enumerate(((grad_gate, keys), (grad_up, keys), (values, hidden))):
        summed = weights[idx].astype(jnp.float32) + dot(left[...], right[...], 0, 0)
        mean = jnp.mean(summed * summed, axis=-1, keepdims=True)
        fresh[idx] = (summed * target[idx] * lax.rsqrt(mean + 1e-06)).astype(jnp.bfloat16)

    query = queries[...]
    gate_pre = dot(query, fresh[0], 1, 1)
    up_pre = dot(query, fresh[1], 1, 1)
    applied = (gate_pre * jax.nn.sigmoid(gate_pre) * up_pre).astype(jnp.bfloat16)
    out = dot(applied, fresh[2], 1, 1).astype(jnp.bfloat16)
    for idx, ref in enumerate(produced):
        ref[...] = out[idx * half : (idx + 1) * half]


def step(place, block, pieces, asked, weights, target):
    half, width = asked[0].shape[1:]
    total = pieces[0].shape[1] * len(pieces)
    tile = 256 if total % 256 == 0 else half
    vmem = pl.BlockSpec(memory_space=pltpu.VMEM)
    anywhere = pl.BlockSpec(memory_space=pltpu.HBM)
    token_buf = pltpu.VMEM((total, width), jnp.bfloat16)
    flops = 2 * width * width * (6 * total + 12 * half)
    outs = pl.pallas_call(
        functools.partial(step_kernel, len(pieces), block, tile),
        in_specs=[pl.BlockSpec(memory_space=pltpu.SMEM)]
        + [anywhere] * (len(pieces) + 4)
        + [vmem, vmem],
        out_specs=[vmem] * 5,
        out_shape=[jax.ShapeDtypeStruct(weights.shape, jnp.bfloat16)]
        + [jax.ShapeDtypeStruct((half, width), jnp.bfloat16)] * 4,
        scratch_shapes=[token_buf] * 5
        + [
            pltpu.VMEM((4 * half, width), jnp.bfloat16),
            pltpu.SemaphoreType.DMA((2 * len(pieces) + 4,)),
        ],
        compiler_params=pltpu.CompilerParams(vmem_limit_bytes=VMEM_LIMIT),
        cost_estimate=pl.CostEstimate(
            flops=flops, bytes_accessed=8 * 1024 * 1024, transcendentals=total * width
        ),
        name="step",
    )(place, *pieces, *asked, weights, target)
    return outs[0], outs[1:]


def place_kernel(place, *refs):
    shard = refs[0]
    slabs = refs[1:9]
    matrix, sems = refs[9:]
    part = slabs[0].shape[1]
    line, core, group = place[1], place[2], place[3]
    rows = pl.ds(pl.multiple_of(line * 4 * part, 4 * part), 4 * part)
    copies = [pltpu.make_async_copy(shard, matrix.at[0, rows], sems.at[8])]
    for idx, slab in enumerate(slabs):
        here_line = line ^ ((idx >> 1) & 1)
        here_group = group ^ (idx & 1)
        here_core = core ^ (idx >> 2)
        at = (here_line * 4 + here_group * 2 + here_core) * part
        rows = pl.ds(pl.multiple_of(at, part), part)
        turns = pl.ds(4 - slab.shape[0], slab.shape[0])
        copies.append(pltpu.make_async_copy(slab, matrix.at[turns, rows], sems.at[idx]))
    for copy in copies:
        copy.start()
    for copy in copies:
        copy.wait()


def place_slabs(place, shard, slabs):
    depth = shard.shape[1]
    anywhere = pl.BlockSpec(memory_space=pltpu.HBM)
    return pl.pallas_call(
        place_kernel,
        in_specs=[pl.BlockSpec(memory_space=pltpu.SMEM)] + [anywhere] * 9,
        out_specs=pl.BlockSpec(memory_space=pltpu.VMEM),
        out_shape=jax.ShapeDtypeStruct((4, 2 * shard.shape[0], depth), jnp.bfloat16),
        scratch_shapes=[pltpu.SemaphoreType.DMA((9,))],
        compiler_params=pltpu.CompilerParams(vmem_limit_bytes=VMEM_LIMIT // 2),
        cost_estimate=pl.CostEstimate(
            flops=0, bytes_accessed=17 * 1024 * 1024, transcendentals=0
        ),
        name="place_slabs",
    )(place, shard, *slabs)


def project_rows(out, mixed, matrix):
    total = None
    for turn in range(4):
        term = dot(mixed[turn][...], matrix[turn], 1, 0)
        total = term if total is None else total + term
    out[...] = total.astype(jnp.bfloat16)


def first_kernel(*refs):
    project_rows(refs[5], refs[:4], refs[4])


def second_kernel(*refs):
    mixed, first, matrix, out = refs[:4], refs[4], refs[5], refs[6]
    out[0] = first[...]
    project_rows(out.at[1], mixed, matrix)


def project(mixed, first, matrix):
    half, width = mixed[0].shape
    depth = matrix.shape[2]
    shape = (half, depth) if first is None else (2, half, depth)
    args = (*mixed, matrix) if first is None else (*mixed, first, matrix)
    vmem = pl.BlockSpec(memory_space=pltpu.VMEM)
    return pl.pallas_call(
        first_kernel if first is None else second_kernel,
        in_specs=[vmem] * len(args),
        out_specs=vmem,
        out_shape=jax.ShapeDtypeStruct(shape, jnp.bfloat16),
        compiler_params=pltpu.CompilerParams(vmem_limit_bytes=VMEM_LIMIT // 2),
        cost_estimate=pl.CostEstimate(
            flops=2 * half * 4 * width * depth, bytes_accessed=9 * 1024 * 1024, transcendentals=0
        ),
        name="project",
    )(*args)


def routes(rule):
    pairs = []
    for row in range(4):
        for line in range(2):
            for core in range(2):
                to_row, to_line, to_core = rule(row, line, core)
                pairs.append(((row * 2 + line) * 2 + core, (to_row * 2 + to_line) * 2 + to_core))
    return pairs


def spread_rule(turn):
    def rule(row, line, core):
        want = row ^ turn
        return (2 * core + (want >> 1), line, want & 1)

    return rule


def swap_line(arr):
    return lax.ppermute(arr, BOTH, routes(lambda row, line, core: (row, 1 - line, core)))


def swap_core(arr):
    return lax.ppermute(arr, BOTH, routes(lambda row, line, core: (row, line, 1 - core)))


def swap_row(arr, turn):
    return lax.ppermute(arr, BOTH, routes(lambda row, line, core: (row ^ turn, line, core)))


def swap_group(arr):
    return lax.ppermute(arr, "groups", [(0, 1), (1, 0)])


def after(arr, *earlier):
    return lax.optimization_barrier((arr,) + earlier)[0]


class Queue:
    def __init__(self, depth):
        self.depth, self.ended = depth, []

    def send(self, swap, arr, *args):
        if len(self.ended) >= self.depth:
            arr = after(arr, self.ended[-self.depth])
        got = swap(arr, *args)
        self.ended.append(got)
        return got


def spread(message, turn):
    return lax.ppermute(message, BOTH, routes(spread_rule(turn)))


def local_gathered(queries, keys, values, rates, fast_init, out_proj):
    seq, core, group = lax.axis_index("seq"), lax.axis_index("head"), lax.axis_index("groups")
    row, line = seq // 2, seq % 2
    place = jnp.stack([row, line, core, group]).astype(jnp.int32)
    rates = rates.transpose(0, 2, 1)
    rows = Queue(2)

    part = out_proj.shape[0] // 4
    quarter = lax.dynamic_slice_in_dim(out_proj, (2 * group + core) * part, part, 0)
    own_line = swap_line(quarter)
    slab_rows = [rows.send(swap_row, quarter, 1)]
    packed = pack(place, queries, keys, values, rates)
    quarter = after(quarter, packed[0][0])
    slab_rows += [rows.send(swap_row, quarter, turn) for turn in (2, 3)]

    arrived = [
        [rows.send(spread, message, turn) for turn, message in enumerate(messages)]
        for messages in packed
    ]
    asked = arrived[2]

    mine = lax.dynamic_index_in_dim(fast_init, row % 2, 1, keepdims=False)
    weights = jnp.where(core == row // 2, mine, swap_core(mine))
    init_float = weights.astype(jnp.float32)
    target = jnp.sqrt(jnp.mean(init_float * init_float, axis=-1, keepdims=True))

    slab = jnp.stack(slab_rows)
    slab_group = swap_group(slab)
    slab_line = jnp.concatenate([own_line[None], swap_line(slab)])
    slab_both = swap_group(slab_line)

    mixed, produced_all, pieces = [], [], []
    for block in range(2):
        own = collect(arrived[block])
        other = swap_line(own)
        pieces.append([own, swap_core(own), other, swap_core(other)])
    for block in range(2):
        weights, produced = step(place, block, pieces[block], asked, weights, target)
        mixed.append(
            [produced[0]] + [rows.send(swap_row, produced[turn], turn) for turn in (1, 2, 3)]
        )
        if block == 0:
            slabs = [slab, slab_group, slab_line, slab_both]
            slabs = slabs + [swap_core(after(arr, pieces[1][0])) for arr in slabs]
    matrix = place_slabs(place, out_proj, slabs)
    return project(mixed[1], project(mixed[0], None, matrix), matrix)


def solution(mesh):
    in_specs = (
        P(None, ("groups", "seq"), "head"),
        P(None, ("groups", "seq"), "head"),
        P(None, ("groups", "seq"), "head"),
        P(None, ("groups", "seq"), "head"),
        P(None, "head", None, None),
        P("seq", None),
    )
    out_specs = P(None, ("groups", "seq", "head"), None)
    few = dict(mesh.shape) == {"groups": 2, "seq": 8, "head": 2}
    local = local_gathered if few else local_summed
    return jax.shard_map(local, mesh=mesh, in_specs=in_specs, out_specs=out_specs, check_vma=False)
```

```python
import functools

import jax
import jax.numpy as jnp
from jax import lax
from jax.experimental import pallas as pl
from jax.experimental.pallas import tpu as pltpu
from jax.sharding import PartitionSpec as P

VMEM_LIMIT = 24 * 1024 * 1024
UPDATE_LIMIT = 60 * 1024 * 1024
BOTH = ("seq", "head")
SMALL = pl.CostEstimate(flops=1, bytes_accessed=1, transcendentals=0)


def silu_parts(value):
    sigma = jax.nn.sigmoid(value)
    return (value * sigma, sigma * (1.0 + value * (1.0 - sigma)))


def dot(left, right, left_dim, right_dim):
    return lax.dot_general(
        left, right, (((left_dim,), (right_dim,)), ((), ())), preferred_element_type=jnp.float32
    )


def local_update(weights, keys_local, values_local, rates_local):
    gate_pre = jnp.einsum(
        "thi,hoi->tho", keys_local, weights[0], preferred_element_type=jnp.float32
    )
    up_pre = jnp.einsum("thi,hoi->tho", keys_local, weights[1], preferred_element_type=jnp.float32)
    gate_act, gate_slope = silu_parts(gate_pre)
    hidden = (gate_act * up_pre).astype(jnp.bfloat16)
    weighted = (rates_local[:, :, None] * values_local.astype(jnp.float32)).astype(jnp.bfloat16)
    back = jnp.einsum("tho,hog->thg", weighted, weights[2], preferred_element_type=jnp.float32)
    grad_gate = (back * up_pre * gate_slope).astype(jnp.bfloat16)
    grad_up = (back * gate_act).astype(jnp.bfloat16)
    return jnp.stack(
        [
            jnp.einsum("thg,thi->hgi", grad_gate, keys_local, preferred_element_type=jnp.float32),
            jnp.einsum("thg,thi->hgi", grad_up, keys_local, preferred_element_type=jnp.float32),
            jnp.einsum("tho,thg->hog", weighted, hidden, preferred_element_type=jnp.float32),
        ]
    )


def apply_local(weights, queries_local):
    gate_pre = jnp.einsum(
        "thi,hoi->tho", queries_local, weights[0], preferred_element_type=jnp.float32
    )
    up_pre = jnp.einsum(
        "thi,hoi->tho", queries_local, weights[1], preferred_element_type=jnp.float32
    )
    gate_act, gate_slope = silu_parts(gate_pre)
    applied = (gate_act * up_pre).astype(jnp.bfloat16)
    produced = jnp.einsum("thg,hog->tho", applied, weights[2], preferred_element_type=jnp.float32)
    return produced.astype(jnp.bfloat16).reshape(queries_local.shape[0], -1)


def local_summed(queries, keys, values, rates, fast_init, out_proj):
    block_count, tok_count, width_here = queries.shape
    heads_here = fast_init.shape[1]
    head_width = fast_init.shape[2]
    init_float = fast_init.astype(jnp.float32)
    target = jnp.sqrt(jnp.mean(init_float * init_float, axis=-1, keepdims=True))
    row_count = head_width // lax.axis_size("seq")
    offset = lax.axis_index("seq") * row_count
    current = fast_init
    produced_list = []
    for block_idx in range(block_count):
        keys_local = keys[block_idx].reshape(tok_count, heads_here, head_width)
        values_local = values[block_idx].reshape(tok_count, heads_here, head_width)
        update = local_update(current, keys_local, values_local, rates[block_idx])
        shard = lax.psum_scatter(update, "seq", scatter_dimension=3, tiled=True)
        own = lax.dynamic_slice_in_dim(current, offset, row_count, 3).astype(jnp.float32) + shard
        squares = lax.psum(jnp.sum(own * own, axis=-1, keepdims=True), "seq")
        fresh = (own * target * lax.rsqrt(squares / head_width + 1e-06)).astype(jnp.bfloat16)
        current = lax.all_gather(fresh, "seq", axis=3, tiled=True)
        produced = apply_local(
            current, queries[block_idx].reshape(tok_count, heads_here, head_width)
        )
        produced_list.append(produced)
    mixed = lax.all_to_all(
        jnp.stack(produced_list), "head", split_axis=1, concat_axis=2, tiled=True
    )
    result = jnp.einsum(
        "ctf,fd->ctd",
        mixed,
        lax.all_gather(out_proj, "seq", axis=0, tiled=True),
        preferred_element_type=jnp.float32,
    )
    return result.astype(jnp.bfloat16)


def pack_kernel(place, queries, keys, values, rates, kept, sent, keys_in, values_in, queries_in, *sems):
    load_sems, out_sems = sems
    half = kept.shape[1]
    blocks = keys_in.shape[0]
    core = place[2]
    loads = []
    for block in range(blocks):
        for source, target in ((values, values_in), (keys, keys_in), (queries, queries_in)):
            sem = load_sems.at[len(loads)]
            loads.append(pltpu.make_async_copy(source.at[block], target.at[block], sem))
            loads[-1].start()
    copies = []

    def send(source, block, slot):
        for out, which in ((sent, 1 - core), (kept, core)):
            rows = pl.ds(pl.multiple_of(which * half, half), half)
            sem = out_sems.at[len(copies)]
            copies.append(pltpu.make_async_copy(source.at[block, rows], out.at[slot], sem))
            copies[-1].start()

    for block in range(blocks):
        for load in loads[3 * block : 3 * block + 3]:
            load.wait()
        send(keys_in, block, 2 * block)
        send(queries_in, block, 2 * blocks + block)
        rate = rates[block].T
        width = keys_in.shape[2] // 2
        for head in range(2):
            cols = slice(head * width, (head + 1) * width)
            scaled = rate[:, head : head + 1] * values_in[block, :, cols].astype(jnp.float32)
            values_in[block, :, cols] = scaled.astype(jnp.bfloat16)
        send(values_in, block, 2 * block + 1)
    for copy in copies:
        copy.wait()


def pack(place, queries, keys, values, rates):
    blocks, tokens, both = keys.shape
    out = jax.ShapeDtypeStruct((3 * blocks, tokens // 2, both), jnp.bfloat16)
    return pl.pallas_call(
        pack_kernel,
        in_specs=[smem(), hbm(), hbm(), hbm(), vmem()],
        out_specs=[pl.BlockSpec(memory_space=pl.ANY)] * 2,
        out_shape=[out, out],
        scratch_shapes=[pltpu.VMEM(keys.shape, jnp.bfloat16)] * 3
        + [pltpu.SemaphoreType.DMA((3 * blocks,)), pltpu.SemaphoreType.DMA((6 * blocks,))],
        cost_estimate=SMALL,
        name="pack",
    )(place, queries, keys, values, rates)


def deal_kernel(place, kept, got, *refs):
    outs, (held, load_sems, sems) = refs[:-3], refs[-3:]
    width = outs[0].shape[3]
    core = place[2]
    loads = [
        pltpu.make_async_copy(kept, held.at[core], load_sems.at[0]),
        pltpu.make_async_copy(got, held.at[1 - core], load_sems.at[1]),
    ]
    for load in loads:
        load.start()
    for load in loads:
        load.wait()
    copies = []
    for idx, out in enumerate(outs):
        for head in range(4):
            source = held.at[head // 2, pl.ds(2 * idx, 2), :, pl.ds((head % 2) * width, width)]
            copies.append(pltpu.make_async_copy(source, out.at[head], sems.at[len(copies)]))
            copies[-1].start()
    for copy in copies:
        copy.wait()


def deal(place, kept, got):
    kinds, half, both = kept.shape
    out = jax.ShapeDtypeStruct((4, 2, half, both // 2), jnp.bfloat16)
    return pl.pallas_call(
        deal_kernel,
        in_specs=[smem(), hbm(), hbm()],
        out_specs=[pl.BlockSpec(memory_space=pl.ANY)] * (kinds // 2),
        out_shape=[out] * (kinds // 2),
        scratch_shapes=[
            pltpu.VMEM((2,) + kept.shape, jnp.bfloat16),
            pltpu.SemaphoreType.DMA((2,)),
            pltpu.SemaphoreType.DMA((2 * kinds,)),
        ],
        cost_estimate=SMALL,
        name="deal",
    )(place, kept, got)


def form_update(pieces, weights, target, fresh, scratch):
    keys, values, hidden, grad_gate, grad_up, sems = scratch
    count, half = pieces[0].shape[0], pieces[0].shape[2]
    copies = []
    for idx, piece in enumerate(pieces):
        for source in range(count):
            rows = pl.ds((count * idx + source) * half, half)
            for kind, buf in enumerate((keys, values)):
                sem = sems.at[len(copies)]
                copies.append(pltpu.make_async_copy(piece.at[source, kind], buf.at[rows], sem))
                copies[-1].start()
    tile = count * half
    for idx in range(len(pieces)):
        for copy in copies[2 * count * idx : 2 * count * (idx + 1)]:
            copy.wait()
        rows = pl.ds(idx * tile, tile)
        key, value = keys[rows], values[rows]
        gate_pre = dot(key, weights[0], 1, 1)
        up_pre = dot(key, weights[1], 1, 1)
        back = dot(value, weights[2], 1, 0)
        gate_act, gate_slope = silu_parts(gate_pre)
        hidden[rows] = (gate_act * up_pre).astype(jnp.bfloat16)
        grad_gate[rows] = (back * up_pre * gate_slope).astype(jnp.bfloat16)
        grad_up[rows] = (back * gate_act).astype(jnp.bfloat16)
    for idx, (left, right) in enumerate(((grad_gate, keys), (grad_up, keys), (values, hidden))):
        summed = weights[idx].astype(jnp.float32) + dot(left[...], right[...], 0, 0)
        mean = jnp.mean(summed * summed, axis=-1, keepdims=True)
        fresh[idx] = (summed * target[idx] * lax.rsqrt(mean + 1e-06)).astype(jnp.bfloat16)


def start_queries(block, place, asked, queries, sems):
    half = asked.shape[2]
    row = place[0]
    copies = []
    for source in range(asked.shape[0]):
        rows = pl.ds(pl.multiple_of((row ^ source) * half, half), half)
        copies.append(
            pltpu.make_async_copy(asked.at[source, block], queries.at[rows], sems.at[source])
        )
        copies[-1].start()
    return copies


def form_outputs(query, weights, produced):
    half = produced[0].shape[0]
    gate_pre = dot(query, weights[0], 1, 1)
    up_pre = dot(query, weights[1], 1, 1)
    applied = (gate_pre * jax.nn.sigmoid(gate_pre) * up_pre).astype(jnp.bfloat16)
    out = dot(applied, weights[2], 1, 1).astype(jnp.bfloat16)
    for idx, ref in enumerate(produced):
        ref[...] = out[idx * half : (idx + 1) * half]


def step_kernel(block, place, *refs):
    pieces, asked, weights, target, fresh = refs[:4], refs[4], refs[5], refs[6], refs[7]
    produced, (queries, query_sems) = refs[8:12], refs[12:14]
    copies = start_queries(block, place, asked, queries, query_sems)
    form_update(pieces, weights, target, fresh, refs[14:])
    for copy in copies:
        copy.wait()
    form_outputs(queries[...], fresh, produced)


def update_kernel(*refs):
    form_update(refs[:4], refs[4], refs[5], refs[6], refs[7:])


def apply_kernel(block, place, *refs):
    asked, weights, produced, queries, sems = refs[0], refs[1], refs[2:6], refs[6], refs[7]
    for copy in start_queries(block, place, asked, queries, sems):
        copy.wait()
    form_outputs(queries[...], weights, produced)


def vmem():
    return pl.BlockSpec(memory_space=pltpu.VMEM)


def hbm():
    return pl.BlockSpec(memory_space=pltpu.HBM)


def smem():
    return pl.BlockSpec(memory_space=pltpu.SMEM)


def update_scratch(pieces):
    count, _, half, width = pieces[0].shape
    buf = pltpu.VMEM((count * len(pieces) * half, width), jnp.bfloat16)
    return [buf] * 5 + [pltpu.SemaphoreType.DMA((2 * count * len(pieces),))]


def query_scratch(asked):
    count, _, half, width = asked.shape
    return [
        pltpu.VMEM((count * half, width), jnp.bfloat16),
        pltpu.SemaphoreType.DMA((count,)),
    ]


def update(pieces, weights, target):
    return pl.pallas_call(
        update_kernel,
        in_specs=[hbm()] * 4 + [vmem(), vmem()],
        out_specs=vmem(),
        out_shape=jax.ShapeDtypeStruct(weights.shape, jnp.bfloat16),
        scratch_shapes=update_scratch(pieces),
        compiler_params=pltpu.CompilerParams(vmem_limit_bytes=UPDATE_LIMIT),
        cost_estimate=SMALL,
        name="update",
    )(*pieces, weights, target)


def apply(place, block, asked, weights):
    return pl.pallas_call(
        functools.partial(apply_kernel, block),
        in_specs=[smem(), hbm(), vmem()],
        out_specs=[vmem()] * 4,
        out_shape=[jax.ShapeDtypeStruct(asked.shape[2:], jnp.bfloat16)] * 4,
        scratch_shapes=query_scratch(asked),
        compiler_params=pltpu.CompilerParams(vmem_limit_bytes=VMEM_LIMIT),
        cost_estimate=SMALL,
        name="apply",
    )(place, asked, weights)


def step(place, block, pieces, asked, weights, target):
    outs = pl.pallas_call(
        functools.partial(step_kernel, block),
        in_specs=[smem()] + [hbm()] * 5 + [vmem(), vmem()],
        out_specs=[vmem()] * 5,
        out_shape=[jax.ShapeDtypeStruct(weights.shape, jnp.bfloat16)]
        + [jax.ShapeDtypeStruct(asked.shape[2:], jnp.bfloat16)] * 4,
        scratch_shapes=query_scratch(asked) + update_scratch(pieces),
        compiler_params=pltpu.CompilerParams(vmem_limit_bytes=UPDATE_LIMIT),
        cost_estimate=SMALL,
        name="step",
    )(place, *pieces, asked, weights, target)
    return outs[1:]


def place_kernel(place, *refs):
    shard, slabs, matrix, sems = refs[0], refs[1:9], refs[9], refs[10]
    part = slabs[0].shape[1]
    line, core, group = place[1], place[2], place[3]
    rows = pl.ds(pl.multiple_of(line * 4 * part, 4 * part), 4 * part)
    copies = [pltpu.make_async_copy(shard, matrix.at[0, rows], sems.at[8])]
    copies[0].start()
    for idx, slab in enumerate(slabs):
        here_line = line ^ ((idx >> 1) & 1)
        here_group = group ^ (idx & 1)
        here_core = core ^ (idx >> 2)
        at = (here_line * 4 + here_group * 2 + here_core) * part
        rows = pl.ds(pl.multiple_of(at, part), part)
        turns = pl.ds(4 - slab.shape[0], slab.shape[0])
        copies.append(pltpu.make_async_copy(slab, matrix.at[turns, rows], sems.at[idx]))
        copies[-1].start()
    for copy in copies:
        copy.wait()


def place_slabs(place, shard, slabs):
    return pl.pallas_call(
        place_kernel,
        in_specs=[smem()] + [hbm()] * 9,
        out_specs=vmem(),
        out_shape=jax.ShapeDtypeStruct((4, 2 * shard.shape[0], shard.shape[1]), jnp.bfloat16),
        scratch_shapes=[pltpu.SemaphoreType.DMA((9,))],
        compiler_params=pltpu.CompilerParams(vmem_limit_bytes=VMEM_LIMIT),
        cost_estimate=SMALL,
        name="place_slabs",
    )(place, shard, *slabs)


def project_rows(out, mixed, matrix):
    total = None
    for turn in range(4):
        term = dot(mixed[turn][...], matrix[turn], 1, 0)
        total = term if total is None else total + term
    out[...] = total.astype(jnp.bfloat16)


def first_kernel(*refs):
    project_rows(refs[5], refs[:4], refs[4])


def second_kernel(*refs):
    mixed, first, matrix, out = refs[:4], refs[4], refs[5], refs[6]
    out[0] = first[...]
    project_rows(out.at[1], mixed, matrix)


def project(mixed, first, matrix):
    half, width = mixed[0].shape
    depth = matrix.shape[2]
    shape = (half, depth) if first is None else (2, half, depth)
    args = (*mixed, matrix) if first is None else (*mixed, first, matrix)
    vmem = pl.BlockSpec(memory_space=pltpu.VMEM)
    return pl.pallas_call(
        first_kernel if first is None else second_kernel,
        in_specs=[vmem] * len(args),
        out_specs=vmem,
        out_shape=jax.ShapeDtypeStruct(shape, jnp.bfloat16),
        compiler_params=pltpu.CompilerParams(vmem_limit_bytes=VMEM_LIMIT),
        cost_estimate=SMALL,
        name="project",
    )(*args)


def routes(rule):
    pairs = []
    for row in range(4):
        for line in range(2):
            for core in range(2):
                to_row, to_line, to_core = rule(row, line, core)
                pairs.append(((row * 2 + line) * 2 + core, (to_row * 2 + to_line) * 2 + to_core))
    return pairs


def swap_line(arr):
    return lax.ppermute(arr, BOTH, routes(lambda row, line, core: (row, 1 - line, core)))


def swap_core(arr):
    return lax.ppermute(arr, BOTH, routes(lambda row, line, core: (row, line, 1 - core)))


def swap_row(arr, turn):
    return lax.ppermute(arr, BOTH, routes(lambda row, line, core: (row ^ turn, line, core)))


def swap_group(arr):
    return lax.ppermute(arr, "groups", [(0, 1), (1, 0)])


def after(arr, *earlier):
    return lax.optimization_barrier((arr,) + earlier)[0]


def exchange(arr):
    groups = [[2 * row + line for row in range(4)] for line in range(2)]
    return lax.all_to_all(arr, "seq", 0, 0, axis_index_groups=groups, tiled=True)


def local_gathered(queries, keys, values, rates, fast_init, out_proj):
    seq, core, group = lax.axis_index("seq"), lax.axis_index("head"), lax.axis_index("groups")
    row, line = seq // 2, seq % 2
    place = jnp.stack([row, line, core, group]).astype(jnp.int32)
    rates = rates.transpose(0, 2, 1)

    part = out_proj.shape[0] // 4
    quarter = lax.dynamic_slice_in_dim(out_proj, (2 * group + core) * part, part, 0)
    own_line = swap_line(quarter)
    slab_rows = [swap_row(quarter, turn) for turn in (1, 2)]
    kept, sent = pack(place, queries, keys, values, rates)
    slab_rows.append(swap_row(after(quarter, kept), 3))
    dealt = deal(place, kept, swap_core(after(sent, own_line, *slab_rows[:2])))

    mine = lax.dynamic_index_in_dim(after(fast_init, kept), row % 2, 1, keepdims=False)
    weights = jnp.where(core == row // 2, mine, swap_core(mine))
    init_float = weights.astype(jnp.float32)
    target = jnp.sqrt(jnp.mean(init_float * init_float, axis=-1, keepdims=True))

    own = exchange(after(dealt[0], target, *slab_rows))
    slab = jnp.stack(slab_rows)
    slab_line = swap_line(slab)
    slab_group = swap_group(slab)
    own_next = exchange(after(dealt[1], slab_line, slab_group, own))
    slab_line = jnp.concatenate([own_line[None], slab_line])
    other = swap_line(own)
    own_core = swap_core(own)
    slab_both = swap_group(slab_line)
    asked = exchange(after(dealt[2], own_next, own_core, other))
    other_next = swap_line(own_next)
    own_next_core = swap_core(own_next)
    first = update([own, own_core, other, swap_core(other)], weights, target)
    produced = apply(place, 0, asked, first)
    mixed = [[produced[0]] + [swap_row(produced[turn], turn) for turn in (1, 2, 3)]]
    other_next_core = swap_core(after(other_next, produced[0]))
    slabs = [slab, slab_group, slab_line, slab_both]
    slabs = slabs + [swap_core(after(arr, first)) for arr in slabs]
    pieces = [own_next, own_next_core, other_next, other_next_core]
    produced = step(place, 1, pieces, asked, after(first, *slabs[4:]), target)
    produced = [produced[0]] + [after(arr, *mixed[0][1:]) for arr in produced[1:]]
    mixed += [[produced[0]] + [swap_row(produced[turn], turn) for turn in (1, 2, 3)]]

    matrix = place_slabs(place, out_proj, slabs)
    return project(mixed[1], project(mixed[0], None, matrix), matrix)


def solution(mesh):
    in_specs = (
        P(None, ("groups", "seq"), "head"),
        P(None, ("groups", "seq"), "head"),
        P(None, ("groups", "seq"), "head"),
        P(None, ("groups", "seq"), "head"),
        P(None, "head", None, None),
        P("seq", None),
    )
    out_specs = P(None, ("groups", "seq", "head"), None)
    few = dict(mesh.shape) == {"groups": 2, "seq": 8, "head": 2}
    local = local_gathered if few else local_summed
    return jax.shard_map(local, mesh=mesh, in_specs=in_specs, out_specs=out_specs, check_vma=False)
```

```python
import functools

import jax
import jax.numpy as jnp
from jax import lax
from jax.experimental import pallas as pl
from jax.experimental.pallas import tpu as pltpu
from jax.sharding import PartitionSpec as P

VMEM_LIMIT = 24 * 1024 * 1024
UPDATE_LIMIT = 32 * 1024 * 1024
BOTH = ("seq", "head")
SMALL = pl.CostEstimate(flops=1, bytes_accessed=1, transcendentals=0)


def silu_parts(value):
    sigma = jax.nn.sigmoid(value)
    return (value * sigma, sigma * (1.0 + value * (1.0 - sigma)))


def dot(left, right, left_dim, right_dim):
    return lax.dot_general(
        left, right, (((left_dim,), (right_dim,)), ((), ())), preferred_element_type=jnp.float32
    )


def local_update(weights, keys_local, values_local, rates_local):
    gate_pre = jnp.einsum(
        "thi,hoi->tho", keys_local, weights[0], preferred_element_type=jnp.float32
    )
    up_pre = jnp.einsum("thi,hoi->tho", keys_local, weights[1], preferred_element_type=jnp.float32)
    gate_act, gate_slope = silu_parts(gate_pre)
    hidden = (gate_act * up_pre).astype(jnp.bfloat16)
    weighted = (rates_local[:, :, None] * values_local.astype(jnp.float32)).astype(jnp.bfloat16)
    back = jnp.einsum("tho,hog->thg", weighted, weights[2], preferred_element_type=jnp.float32)
    grad_gate = (back * up_pre * gate_slope).astype(jnp.bfloat16)
    grad_up = (back * gate_act).astype(jnp.bfloat16)
    return jnp.stack(
        [
            jnp.einsum("thg,thi->hgi", grad_gate, keys_local, preferred_element_type=jnp.float32),
            jnp.einsum("thg,thi->hgi", grad_up, keys_local, preferred_element_type=jnp.float32),
            jnp.einsum("tho,thg->hog", weighted, hidden, preferred_element_type=jnp.float32),
        ]
    )


def apply_local(weights, queries_local):
    gate_pre = jnp.einsum(
        "thi,hoi->tho", queries_local, weights[0], preferred_element_type=jnp.float32
    )
    up_pre = jnp.einsum(
        "thi,hoi->tho", queries_local, weights[1], preferred_element_type=jnp.float32
    )
    gate_act, gate_slope = silu_parts(gate_pre)
    applied = (gate_act * up_pre).astype(jnp.bfloat16)
    produced = jnp.einsum("thg,hog->tho", applied, weights[2], preferred_element_type=jnp.float32)
    return produced.astype(jnp.bfloat16).reshape(queries_local.shape[0], -1)


def local_summed(queries, keys, values, rates, fast_init, out_proj):
    block_count, tok_count, width_here = queries.shape
    heads_here = fast_init.shape[1]
    head_width = fast_init.shape[2]
    init_float = fast_init.astype(jnp.float32)
    target = jnp.sqrt(jnp.mean(init_float * init_float, axis=-1, keepdims=True))
    row_count = head_width // lax.axis_size("seq")
    offset = lax.axis_index("seq") * row_count
    current = fast_init
    produced_list = []
    for block_idx in range(block_count):
        keys_local = keys[block_idx].reshape(tok_count, heads_here, head_width)
        values_local = values[block_idx].reshape(tok_count, heads_here, head_width)
        update = local_update(current, keys_local, values_local, rates[block_idx])
        shard = lax.psum_scatter(update, "seq", scatter_dimension=3, tiled=True)
        own = lax.dynamic_slice_in_dim(current, offset, row_count, 3).astype(jnp.float32) + shard
        squares = lax.psum(jnp.sum(own * own, axis=-1, keepdims=True), "seq")
        fresh = (own * target * lax.rsqrt(squares / head_width + 1e-06)).astype(jnp.bfloat16)
        current = lax.all_gather(fresh, "seq", axis=3, tiled=True)
        produced = apply_local(
            current, queries[block_idx].reshape(tok_count, heads_here, head_width)
        )
        produced_list.append(produced)
    mixed = lax.all_to_all(
        jnp.stack(produced_list), "head", split_axis=1, concat_axis=2, tiled=True
    )
    result = jnp.einsum(
        "ctf,fd->ctd",
        mixed,
        lax.all_gather(out_proj, "seq", axis=0, tiled=True),
        preferred_element_type=jnp.float32,
    )
    return result.astype(jnp.bfloat16)


def pack_kernel(place, queries, keys, values, rates, kept, sent, keys_in, values_in, queries_in, *sems):
    load_sems, out_sems = sems
    half = kept.shape[1]
    blocks = keys_in.shape[0]
    core = place[2]
    loads = []
    for block in range(blocks):
        for source, target in ((values, values_in), (keys, keys_in), (queries, queries_in)):
            sem = load_sems.at[len(loads)]
            loads.append(pltpu.make_async_copy(source.at[block], target.at[block], sem))
            loads[-1].start()
    copies = []

    def send(source, block, slot):
        for out, which in ((sent, 1 - core), (kept, core)):
            rows = pl.ds(pl.multiple_of(which * half, half), half)
            sem = out_sems.at[len(copies)]
            copies.append(pltpu.make_async_copy(source.at[block, rows], out.at[slot], sem))
            copies[-1].start()

    for block in range(blocks):
        for load in loads[3 * block : 3 * block + 3]:
            load.wait()
        send(keys_in, block, 2 * block)
        send(queries_in, block, 2 * blocks + block)
        rate = rates[block].T
        width = keys_in.shape[2] // 2
        for head in range(2):
            cols = slice(head * width, (head + 1) * width)
            scaled = rate[:, head : head + 1] * values_in[block, :, cols].astype(jnp.float32)
            values_in[block, :, cols] = scaled.astype(jnp.bfloat16)
        send(values_in, block, 2 * block + 1)
    for copy in copies:
        copy.wait()


def pack(place, queries, keys, values, rates):
    blocks, tokens, both = keys.shape
    out = jax.ShapeDtypeStruct((3 * blocks, tokens // 2, both), jnp.bfloat16)
    return pl.pallas_call(
        pack_kernel,
        in_specs=[smem(), hbm(), hbm(), hbm(), vmem()],
        out_specs=[pl.BlockSpec(memory_space=pl.ANY)] * 2,
        out_shape=[out, out],
        scratch_shapes=[pltpu.VMEM(keys.shape, jnp.bfloat16)] * 3
        + [pltpu.SemaphoreType.DMA((3 * blocks,)), pltpu.SemaphoreType.DMA((6 * blocks,))],
        cost_estimate=SMALL,
        name="pack",
    )(place, queries, keys, values, rates)


def deal_kernel(place, kept, got, *refs):
    outs, (held, load_sems, sems) = refs[:-3], refs[-3:]
    width = outs[0].shape[3]
    core = place[2]
    loads = [
        pltpu.make_async_copy(kept, held.at[core], load_sems.at[0]),
        pltpu.make_async_copy(got, held.at[1 - core], load_sems.at[1]),
    ]
    for load in loads:
        load.start()
    for load in loads:
        load.wait()
    copies = []
    for idx, out in enumerate(outs):
        for head in range(4):
            source = held.at[head // 2, pl.ds(2 * idx, 2), :, pl.ds((head % 2) * width, width)]
            copies.append(pltpu.make_async_copy(source, out.at[head], sems.at[len(copies)]))
            copies[-1].start()
    for copy in copies:
        copy.wait()


def deal(place, kept, got):
    kinds, half, both = kept.shape
    out = jax.ShapeDtypeStruct((4, 2, half, both // 2), jnp.bfloat16)
    return pl.pallas_call(
        deal_kernel,
        in_specs=[smem(), hbm(), hbm()],
        out_specs=[pl.BlockSpec(memory_space=pl.ANY)] * (kinds // 2),
        out_shape=[out] * (kinds // 2),
        scratch_shapes=[
            pltpu.VMEM((2,) + kept.shape, jnp.bfloat16),
            pltpu.SemaphoreType.DMA((2,)),
            pltpu.SemaphoreType.DMA((2 * kinds,)),
        ],
        cost_estimate=SMALL,
        name="deal",
    )(place, kept, got)


def start_pieces(pieces, scratch):
    keys, values, sems = scratch[0], scratch[1], scratch[5]
    count, half = pieces[0].shape[0], pieces[0].shape[2]
    copies = []
    for idx, piece in enumerate(pieces):
        for source in range(count):
            rows = pl.ds((count * idx + source) * half, half)
            for kind, buf in enumerate((keys, values)):
                sem = sems.at[len(copies)]
                copies.append(pltpu.make_async_copy(piece.at[source, kind], buf.at[rows], sem))
                copies[-1].start()
    return copies


def form_update(copies, count, weights, target, fresh, scratch):
    keys, values, hidden, grad_gate, grad_up, _ = scratch
    tile, share = keys.shape[0] // count, len(copies) // count
    for idx in range(count):
        for copy in copies[share * idx : share * (idx + 1)]:
            copy.wait()
        rows = pl.ds(idx * tile, tile)
        key, value = keys[rows], values[rows]
        gate_pre = dot(key, weights[0], 1, 1)
        up_pre = dot(key, weights[1], 1, 1)
        back = dot(value, weights[2], 1, 0)
        gate_act, gate_slope = silu_parts(gate_pre)
        hidden[rows] = (gate_act * up_pre).astype(jnp.bfloat16)
        grad_gate[rows] = (back * up_pre * gate_slope).astype(jnp.bfloat16)
        grad_up[rows] = (back * gate_act).astype(jnp.bfloat16)
    for idx, (left, right) in enumerate(((grad_gate, keys), (grad_up, keys), (values, hidden))):
        summed = weights[idx].astype(jnp.float32) + dot(left[...], right[...], 0, 0)
        mean = jnp.mean(summed * summed, axis=-1, keepdims=True)
        fresh[idx] = (summed * target[idx] * lax.rsqrt(mean + 1e-06)).astype(jnp.bfloat16)


def start_queries(block, place, asked, queries, sems):
    half = asked.shape[2]
    row = place[0]
    copies = []
    for source in range(asked.shape[0]):
        rows = pl.ds(pl.multiple_of((row ^ source) * half, half), half)
        copies.append(
            pltpu.make_async_copy(asked.at[source, block], queries.at[rows], sems.at[source])
        )
        copies[-1].start()
    return copies


def form_outputs(query, weights, produced):
    half = produced[0].shape[0]
    gate_pre = dot(query, weights[0], 1, 1)
    up_pre = dot(query, weights[1], 1, 1)
    applied = (gate_pre * jax.nn.sigmoid(gate_pre) * up_pre).astype(jnp.bfloat16)
    out = dot(applied, weights[2], 1, 1).astype(jnp.bfloat16)
    for idx, ref in enumerate(produced):
        ref[...] = out[idx * half : (idx + 1) * half]


def step_kernel(block, place, *refs):
    pieces, asked, weights, target, fresh = refs[:4], refs[4], refs[5], refs[6], refs[7]
    produced, (queries, query_sems) = refs[8:12], refs[12:14]
    copies = start_queries(block, place, asked, queries, query_sems)
    form_update(start_pieces(pieces, refs[14:]), 4, weights, target, fresh, refs[14:])
    for copy in copies:
        copy.wait()
    form_outputs(queries[...], fresh, produced)


def first_kernel(place, *refs):
    pieces = refs[:4]
    held, swapped, fresh, target, weights, sem = refs[4:10]
    row, core = place[0], place[2]

    def load(source):
        copy = pltpu.make_async_copy(source.at[:, row % 2], weights, sem.at[0])
        copy.start()
        copy.wait()

    copies = start_pieces(pieces, refs[10:])

    @pl.when(core == row // 2)
    def _():
        load(held)

    @pl.when(core != row // 2)
    def _():
        load(swapped)

    for idx in range(weights.shape[0]):
        init = weights[idx].astype(jnp.float32)
        target[idx] = jnp.sqrt(jnp.mean(init * init, axis=-1, keepdims=True))
    form_update(copies, 4, weights, target, fresh, refs[10:])


def apply_kernel(block, place, *refs):
    asked, weights, produced, queries, sems = refs[0], refs[1], refs[2:6], refs[6], refs[7]
    for copy in start_queries(block, place, asked, queries, sems):
        copy.wait()
    form_outputs(queries[...], weights, produced)


def vmem():
    return pl.BlockSpec(memory_space=pltpu.VMEM)


def hbm():
    return pl.BlockSpec(memory_space=pltpu.HBM)


def smem():
    return pl.BlockSpec(memory_space=pltpu.SMEM)


def update_scratch(pieces):
    count, _, half, width = pieces[0].shape
    buf = pltpu.VMEM((count * len(pieces) * half, width), jnp.bfloat16)
    return [buf] * 5 + [pltpu.SemaphoreType.DMA((2 * count * len(pieces),))]


def query_scratch(asked):
    count, _, half, width = asked.shape
    return [
        pltpu.VMEM((count * half, width), jnp.bfloat16),
        pltpu.SemaphoreType.DMA((count,)),
    ]


def first_update(place, pieces, held, swapped):
    kinds, _, rows, cols = held.shape
    return pl.pallas_call(
        first_kernel,
        in_specs=[smem()] + [hbm()] * 6,
        out_specs=[vmem(), vmem()],
        out_shape=[
            jax.ShapeDtypeStruct((kinds, rows, cols), jnp.bfloat16),
            jax.ShapeDtypeStruct((kinds, rows, 1), jnp.float32),
        ],
        scratch_shapes=[
            pltpu.VMEM((kinds, rows, cols), jnp.bfloat16),
            pltpu.SemaphoreType.DMA((1,)),
        ]
        + update_scratch(pieces),
        compiler_params=pltpu.CompilerParams(vmem_limit_bytes=UPDATE_LIMIT),
        cost_estimate=SMALL,
        name="first_update",
    )(place, *pieces, held, swapped)


def apply(place, block, asked, weights):
    return pl.pallas_call(
        functools.partial(apply_kernel, block),
        in_specs=[smem(), hbm(), vmem()],
        out_specs=[vmem()] * 4,
        out_shape=[jax.ShapeDtypeStruct(asked.shape[2:], jnp.bfloat16)] * 4,
        scratch_shapes=query_scratch(asked),
        compiler_params=pltpu.CompilerParams(vmem_limit_bytes=VMEM_LIMIT),
        cost_estimate=SMALL,
        name="apply",
    )(place, asked, weights)


def step(place, block, pieces, asked, weights, target):
    outs = pl.pallas_call(
        functools.partial(step_kernel, block),
        in_specs=[smem()] + [hbm()] * 5 + [vmem(), vmem()],
        out_specs=[vmem()] * 5,
        out_shape=[jax.ShapeDtypeStruct(weights.shape, jnp.bfloat16)]
        + [jax.ShapeDtypeStruct(asked.shape[2:], jnp.bfloat16)] * 4,
        scratch_shapes=query_scratch(asked) + update_scratch(pieces),
        compiler_params=pltpu.CompilerParams(vmem_limit_bytes=UPDATE_LIMIT),
        cost_estimate=SMALL,
        name="step",
    )(place, *pieces, asked, weights, target)
    return outs[1:]


def place_kernel(place, *refs):
    slabs, matrix, sems = refs[:8], refs[8], refs[9]
    part = slabs[0].shape[1]
    line, core, group = place[1], place[2], place[3]
    copies = []
    for idx, slab in enumerate(slabs):
        here_line = line ^ ((idx >> 1) & 1)
        here_group = group ^ (idx & 1)
        here_core = core ^ (idx >> 2)
        at = (here_line * 4 + here_group * 2 + here_core) * part
        rows = pl.ds(pl.multiple_of(at, part), part)
        copies.append(pltpu.make_async_copy(slab, matrix.at[:, rows], sems.at[idx]))
        copies[-1].start()
    for copy in copies:
        copy.wait()


def place_slabs(place, slabs):
    count, part, depth = slabs[0].shape
    return pl.pallas_call(
        place_kernel,
        in_specs=[smem()] + [hbm()] * 8,
        out_specs=vmem(),
        out_shape=jax.ShapeDtypeStruct((count, 8 * part, depth), jnp.bfloat16),
        scratch_shapes=[pltpu.SemaphoreType.DMA((8,))],
        compiler_params=pltpu.CompilerParams(vmem_limit_bytes=VMEM_LIMIT),
        cost_estimate=SMALL,
        name="place_slabs",
    )(place, *slabs)


def project_rows(row, out, mixed, matrix):
    total = None
    for turn in range(4):
        term = dot(mixed[turn][...], matrix[row ^ turn], 1, 0)
        total = term if total is None else total + term
    out[...] = total.astype(jnp.bfloat16)


def project_first(place, *refs):
    project_rows(place[0], refs[5], refs[:4], refs[4])


def project_second(place, *refs):
    mixed, first, matrix, out = refs[:4], refs[4], refs[5], refs[6]
    out[0] = first[...]
    project_rows(place[0], out.at[1], mixed, matrix)


def project(place, mixed, first, matrix):
    half = mixed[0].shape[0]
    depth = matrix.shape[2]
    shape = (half, depth) if first is None else (2, half, depth)
    args = (*mixed, matrix) if first is None else (*mixed, first, matrix)
    return pl.pallas_call(
        project_first if first is None else project_second,
        in_specs=[smem()] + [vmem()] * len(args),
        out_specs=vmem(),
        out_shape=jax.ShapeDtypeStruct(shape, jnp.bfloat16),
        compiler_params=pltpu.CompilerParams(vmem_limit_bytes=VMEM_LIMIT),
        cost_estimate=SMALL,
        name="project",
    )(place, *args)


def routes(rule):
    pairs = []
    for row in range(4):
        for line in range(2):
            for core in range(2):
                to_row, to_line, to_core = rule(row, line, core)
                pairs.append(((row * 2 + line) * 2 + core, (to_row * 2 + to_line) * 2 + to_core))
    return pairs


def swap_line(arr):
    return lax.ppermute(arr, BOTH, routes(lambda row, line, core: (row, 1 - line, core)))


def swap_core(arr):
    return lax.ppermute(arr, BOTH, routes(lambda row, line, core: (row, line, 1 - core)))


def swap_row(arr, turn):
    return lax.ppermute(arr, BOTH, routes(lambda row, line, core: (row ^ turn, line, core)))


def swap_group(arr):
    return lax.ppermute(arr, "groups", [(0, 1), (1, 0)])


def after(arr, *earlier):
    return lax.optimization_barrier((arr,) + earlier)[0]


def exchange(arr):
    groups = [[2 * row + line for row in range(4)] for line in range(2)]
    return lax.all_to_all(arr, "seq", 0, 0, axis_index_groups=groups, tiled=True)


def local_gathered(queries, keys, values, rates, fast_init, out_proj):
    seq, core, group = lax.axis_index("seq"), lax.axis_index("head"), lax.axis_index("groups")
    row, line = seq // 2, seq % 2
    place = jnp.stack([row, line, core, group]).astype(jnp.int32)
    rates = rates.transpose(0, 2, 1)

    part = out_proj.shape[0] // 4
    quarter = lax.dynamic_slice_in_dim(out_proj, (2 * group + core) * part, part, 0)
    quarters = jnp.broadcast_to(quarter[None], (4,) + quarter.shape)
    slab = exchange(quarters)
    kept, sent = pack(place, after(queries, quarters), keys, values, rates)
    dealt = deal(place, kept, swap_core(sent))
    swapped = swap_core(fast_init)

    own = exchange(after(dealt[0], swapped, slab))
    slab_line = swap_line(slab)
    slab_group = swap_group(slab)
    own_next = exchange(after(dealt[1], own))
    other = swap_line(after(own, slab_line, slab_group))
    own_core = swap_core(own)
    slab_both = swap_group(slab_line)
    asked = exchange(after(dealt[2], own_next, own_core, other))
    other_next = swap_line(own_next)
    own_next_core = swap_core(own_next)
    first, target = first_update(
        place, [own, own_core, other, swap_core(other)], fast_init, swapped
    )
    produced = apply(place, 0, asked, first)
    mixed = [[produced[0]] + [swap_row(produced[turn], turn) for turn in (1, 2, 3)]]
    other_next_core = swap_core(after(other_next, first))
    slabs = [slab, slab_group, slab_line, slab_both]
    slabs = slabs + [swap_core(after(arr, own_next)) for arr in slabs]
    pieces = [own_next, own_next_core, other_next, other_next_core]
    produced = step(place, 1, pieces, asked, after(first, *slabs[4:]), target)
    produced = [produced[0]] + [after(arr, *mixed[0][1:]) for arr in produced[1:]]
    mixed += [[produced[0]] + [swap_row(produced[turn], turn) for turn in (1, 2, 3)]]

    matrix = place_slabs(place, slabs)
    return project(place, mixed[1], project(place, mixed[0], None, matrix), matrix)


def solution(mesh):
    in_specs = (
        P(None, ("groups", "seq"), "head"),
        P(None, ("groups", "seq"), "head"),
        P(None, ("groups", "seq"), "head"),
        P(None, ("groups", "seq"), "head"),
        P(None, "head", None, None),
        P("seq", None),
    )
    out_specs = P(None, ("groups", "seq", "head"), None)
    few = dict(mesh.shape) == {"groups": 2, "seq": 8, "head": 2}
    local = local_gathered if few else local_summed
    return jax.shard_map(local, mesh=mesh, in_specs=in_specs, out_specs=out_specs, check_vma=False)
```

```python
import functools

import jax
import jax.numpy as jnp
from jax import lax
from jax.experimental import pallas as pl
from jax.experimental.pallas import tpu as pltpu
from jax.sharding import PartitionSpec as P

VMEM_LIMIT = 24 * 1024 * 1024
UPDATE_LIMIT = 45 * 1024 * 1024
BOTH = ("seq", "head")
SMALL = pl.CostEstimate(flops=1, bytes_accessed=1, transcendentals=0)


def silu_parts(value):
    sigma = jax.nn.sigmoid(value)
    return (value * sigma, sigma * (1.0 + value * (1.0 - sigma)))


def dot(left, right, left_dim, right_dim):
    return lax.dot_general(
        left, right, (((left_dim,), (right_dim,)), ((), ())), preferred_element_type=jnp.float32
    )


def local_update(weights, keys_local, values_local, rates_local):
    gate_pre = jnp.einsum(
        "thi,hoi->tho", keys_local, weights[0], preferred_element_type=jnp.float32
    )
    up_pre = jnp.einsum("thi,hoi->tho", keys_local, weights[1], preferred_element_type=jnp.float32)
    gate_act, gate_slope = silu_parts(gate_pre)
    hidden = (gate_act * up_pre).astype(jnp.bfloat16)
    weighted = (rates_local[:, :, None] * values_local.astype(jnp.float32)).astype(jnp.bfloat16)
    back = jnp.einsum("tho,hog->thg", weighted, weights[2], preferred_element_type=jnp.float32)
    grad_gate = (back * up_pre * gate_slope).astype(jnp.bfloat16)
    grad_up = (back * gate_act).astype(jnp.bfloat16)
    return jnp.stack(
        [
            jnp.einsum("thg,thi->hgi", grad_gate, keys_local, preferred_element_type=jnp.float32),
            jnp.einsum("thg,thi->hgi", grad_up, keys_local, preferred_element_type=jnp.float32),
            jnp.einsum("tho,thg->hog", weighted, hidden, preferred_element_type=jnp.float32),
        ]
    )


def apply_local(weights, queries_local):
    gate_pre = jnp.einsum(
        "thi,hoi->tho", queries_local, weights[0], preferred_element_type=jnp.float32
    )
    up_pre = jnp.einsum(
        "thi,hoi->tho", queries_local, weights[1], preferred_element_type=jnp.float32
    )
    gate_act, gate_slope = silu_parts(gate_pre)
    applied = (gate_act * up_pre).astype(jnp.bfloat16)
    produced = jnp.einsum("thg,hog->tho", applied, weights[2], preferred_element_type=jnp.float32)
    return produced.astype(jnp.bfloat16).reshape(queries_local.shape[0], -1)


def local_summed(queries, keys, values, rates, fast_init, out_proj):
    block_count, tok_count, width_here = queries.shape
    heads_here = fast_init.shape[1]
    head_width = fast_init.shape[2]
    init_float = fast_init.astype(jnp.float32)
    target = jnp.sqrt(jnp.mean(init_float * init_float, axis=-1, keepdims=True))
    row_count = head_width // lax.axis_size("seq")
    offset = lax.axis_index("seq") * row_count
    current = fast_init
    produced_list = []
    for block_idx in range(block_count):
        keys_local = keys[block_idx].reshape(tok_count, heads_here, head_width)
        values_local = values[block_idx].reshape(tok_count, heads_here, head_width)
        update = local_update(current, keys_local, values_local, rates[block_idx])
        shard = lax.psum_scatter(update, "seq", scatter_dimension=3, tiled=True)
        own = lax.dynamic_slice_in_dim(current, offset, row_count, 3).astype(jnp.float32) + shard
        squares = lax.psum(jnp.sum(own * own, axis=-1, keepdims=True), "seq")
        fresh = (own * target * lax.rsqrt(squares / head_width + 1e-06)).astype(jnp.bfloat16)
        current = lax.all_gather(fresh, "seq", axis=3, tiled=True)
        produced = apply_local(
            current, queries[block_idx].reshape(tok_count, heads_here, head_width)
        )
        produced_list.append(produced)
    mixed = lax.all_to_all(
        jnp.stack(produced_list), "head", split_axis=1, concat_axis=2, tiled=True
    )
    result = jnp.einsum(
        "ctf,fd->ctd",
        mixed,
        lax.all_gather(out_proj, "seq", axis=0, tiled=True),
        preferred_element_type=jnp.float32,
    )
    return result.astype(jnp.bfloat16)


def pack_kernel(place, queries, keys, values, rates, kept, sent, keys_in, values_in, queries_in, *sems):
    load_sems, out_sems = sems
    half = kept.shape[1]
    blocks = keys_in.shape[0]
    core = place[2]
    loads = []
    for block in range(blocks):
        for source, target in ((values, values_in), (keys, keys_in), (queries, queries_in)):
            sem = load_sems.at[len(loads)]
            loads.append(pltpu.make_async_copy(source.at[block], target.at[block], sem))
            loads[-1].start()
    copies = []

    def send(source, block, slot):
        for out, which in ((sent, 1 - core), (kept, core)):
            rows = pl.ds(pl.multiple_of(which * half, half), half)
            sem = out_sems.at[len(copies)]
            copies.append(pltpu.make_async_copy(source.at[block, rows], out.at[slot], sem))
            copies[-1].start()

    for block in range(blocks):
        for load in loads[3 * block : 3 * block + 3]:
            load.wait()
        send(keys_in, block, 2 * block)
        send(queries_in, block, 2 * blocks + block)
        rate = rates[block].T
        width = keys_in.shape[2] // 2
        for head in range(2):
            cols = slice(head * width, (head + 1) * width)
            scaled = rate[:, head : head + 1] * values_in[block, :, cols].astype(jnp.float32)
            values_in[block, :, cols] = scaled.astype(jnp.bfloat16)
        send(values_in, block, 2 * block + 1)
    for copy in copies:
        copy.wait()


def pack(place, queries, keys, values, rates):
    blocks, tokens, both = keys.shape
    out = jax.ShapeDtypeStruct((3 * blocks, tokens // 2, both), jnp.bfloat16)
    return pl.pallas_call(
        pack_kernel,
        in_specs=[smem(), hbm(), hbm(), hbm(), vmem()],
        out_specs=[pl.BlockSpec(memory_space=pl.ANY)] * 2,
        out_shape=[out, out],
        scratch_shapes=[pltpu.VMEM(keys.shape, jnp.bfloat16)] * 3
        + [pltpu.SemaphoreType.DMA((3 * blocks,)), pltpu.SemaphoreType.DMA((6 * blocks,))],
        cost_estimate=SMALL,
        name="pack",
    )(place, queries, keys, values, rates)


def deal_kernel(place, kept, got, *refs):
    outs, (held, load_sems, sems) = refs[:-3], refs[-3:]
    width = outs[0].shape[3]
    core = place[2]
    loads = [
        pltpu.make_async_copy(kept, held.at[core], load_sems.at[0]),
        pltpu.make_async_copy(got, held.at[1 - core], load_sems.at[1]),
    ]
    for load in loads:
        load.start()
    for load in loads:
        load.wait()
    copies = []
    for idx, out in enumerate(outs):
        for head in range(4):
            source = held.at[head // 2, pl.ds(2 * idx, 2), :, pl.ds((head % 2) * width, width)]
            copies.append(pltpu.make_async_copy(source, out.at[head], sems.at[len(copies)]))
            copies[-1].start()
    for copy in copies:
        copy.wait()


def deal(place, kept, got):
    kinds, half, both = kept.shape
    out = jax.ShapeDtypeStruct((4, 2, half, both // 2), jnp.bfloat16)
    return pl.pallas_call(
        deal_kernel,
        in_specs=[smem(), hbm(), hbm()],
        out_specs=[pl.BlockSpec(memory_space=pl.ANY)] * (kinds // 2),
        out_shape=[out] * (kinds // 2),
        scratch_shapes=[
            pltpu.VMEM((2,) + kept.shape, jnp.bfloat16),
            pltpu.SemaphoreType.DMA((2,)),
            pltpu.SemaphoreType.DMA((2 * kinds,)),
        ],
        cost_estimate=SMALL,
        name="deal",
    )(place, kept, got)


def start_pieces(pieces, scratch):
    keys, values, sems = scratch[0], scratch[1], scratch[5]
    count, half = pieces[0].shape[0], pieces[0].shape[2]
    copies = []
    for idx, piece in enumerate(pieces):
        for source in range(count):
            rows = pl.ds((count * idx + source) * half, half)
            for kind, buf in enumerate((keys, values)):
                sem = sems.at[len(copies)]
                copies.append(pltpu.make_async_copy(piece.at[source, kind], buf.at[rows], sem))
                copies[-1].start()
    return copies


def form_update(copies, count, weights, target, fresh, scratch):
    keys, values, hidden, grad_gate, grad_up, _ = scratch
    tile, share = keys.shape[0] // count, len(copies) // count
    for idx in range(count):
        for copy in copies[share * idx : share * (idx + 1)]:
            copy.wait()
        rows = pl.ds(idx * tile, tile)
        key, value = keys[rows], values[rows]
        gate_pre = dot(key, weights[0], 1, 1)
        up_pre = dot(key, weights[1], 1, 1)
        back = dot(value, weights[2], 1, 0)
        gate_act, gate_slope = silu_parts(gate_pre)
        hidden[rows] = (gate_act * up_pre).astype(jnp.bfloat16)
        grad_gate[rows] = (back * up_pre * gate_slope).astype(jnp.bfloat16)
        grad_up[rows] = (back * gate_act).astype(jnp.bfloat16)
    for idx, (left, right) in enumerate(((grad_gate, keys), (grad_up, keys), (values, hidden))):
        summed = weights[idx].astype(jnp.float32) + dot(left[...], right[...], 0, 0)
        mean = jnp.mean(summed * summed, axis=-1, keepdims=True)
        fresh[idx] = (summed * target[idx] * lax.rsqrt(mean + 1e-06)).astype(jnp.bfloat16)


def start_queries(block, place, asked, queries, sems):
    half = asked.shape[2]
    row = place[0]
    copies = []
    for source in range(asked.shape[0]):
        rows = pl.ds(pl.multiple_of((row ^ source) * half, half), half)
        copies.append(
            pltpu.make_async_copy(asked.at[source, block], queries.at[rows], sems.at[source])
        )
        copies[-1].start()
    return copies


def form_outputs(query, weights, produced):
    half = produced[0].shape[0]
    gate_pre = dot(query, weights[0], 1, 1)
    up_pre = dot(query, weights[1], 1, 1)
    applied = (gate_pre * jax.nn.sigmoid(gate_pre) * up_pre).astype(jnp.bfloat16)
    out = dot(applied, weights[2], 1, 1).astype(jnp.bfloat16)
    for idx, ref in enumerate(produced):
        ref[...] = out[idx * half : (idx + 1) * half]


def step_kernel(block, place, *refs):
    pieces, asked, weights, target, fresh = refs[:4], refs[4], refs[5], refs[6], refs[7]
    produced, (queries, query_sems) = refs[8:12], refs[12:14]
    copies = start_queries(block, place, asked, queries, query_sems)
    form_update(start_pieces(pieces, refs[14:]), 2, weights, target, fresh, refs[14:])
    for copy in copies:
        copy.wait()
    form_outputs(queries[...], fresh, produced)


def first_kernel(place, *refs):
    pieces = refs[:4]
    held, swapped, fresh, target, weights, sem = refs[4:10]
    row, core = place[0], place[2]

    def load(source):
        copy = pltpu.make_async_copy(source.at[:, row % 2], weights, sem.at[0])
        copy.start()
        copy.wait()

    copies = start_pieces(pieces, refs[10:])

    @pl.when(core == row // 2)
    def _():
        load(held)

    @pl.when(core != row // 2)
    def _():
        load(swapped)

    for idx in range(weights.shape[0]):
        init = weights[idx].astype(jnp.float32)
        target[idx] = jnp.sqrt(jnp.mean(init * init, axis=-1, keepdims=True))
    form_update(copies, 2, weights, target, fresh, refs[10:])


def apply_kernel(block, place, *refs):
    asked, weights, produced, queries, sems = refs[0], refs[1], refs[2:6], refs[6], refs[7]
    for copy in start_queries(block, place, asked, queries, sems):
        copy.wait()
    form_outputs(queries[...], weights, produced)


def vmem():
    return pl.BlockSpec(memory_space=pltpu.VMEM)


def hbm():
    return pl.BlockSpec(memory_space=pltpu.HBM)


def smem():
    return pl.BlockSpec(memory_space=pltpu.SMEM)


def update_scratch(pieces):
    count, _, half, width = pieces[0].shape
    buf = pltpu.VMEM((count * len(pieces) * half, width), jnp.bfloat16)
    return [buf] * 5 + [pltpu.SemaphoreType.DMA((2 * count * len(pieces),))]


def query_scratch(asked):
    count, _, half, width = asked.shape
    return [
        pltpu.VMEM((count * half, width), jnp.bfloat16),
        pltpu.SemaphoreType.DMA((count,)),
    ]


def first_update(place, pieces, held, swapped):
    kinds, _, rows, cols = held.shape
    return pl.pallas_call(
        first_kernel,
        in_specs=[smem()] + [hbm()] * 6,
        out_specs=[vmem(), vmem()],
        out_shape=[
            jax.ShapeDtypeStruct((kinds, rows, cols), jnp.bfloat16),
            jax.ShapeDtypeStruct((kinds, rows, 1), jnp.float32),
        ],
        scratch_shapes=[
            pltpu.VMEM((kinds, rows, cols), jnp.bfloat16),
            pltpu.SemaphoreType.DMA((1,)),
        ]
        + update_scratch(pieces),
        compiler_params=pltpu.CompilerParams(vmem_limit_bytes=UPDATE_LIMIT),
        cost_estimate=SMALL,
        name="first_update",
    )(place, *pieces, held, swapped)


def apply(place, block, asked, weights):
    return pl.pallas_call(
        functools.partial(apply_kernel, block),
        in_specs=[smem(), hbm(), vmem()],
        out_specs=[vmem()] * 4,
        out_shape=[jax.ShapeDtypeStruct(asked.shape[2:], jnp.bfloat16)] * 4,
        scratch_shapes=query_scratch(asked),
        compiler_params=pltpu.CompilerParams(vmem_limit_bytes=VMEM_LIMIT),
        cost_estimate=SMALL,
        name="apply",
    )(place, asked, weights)


def step(place, block, pieces, asked, weights, target):
    outs = pl.pallas_call(
        functools.partial(step_kernel, block),
        in_specs=[smem()] + [hbm()] * 5 + [vmem(), vmem()],
        out_specs=[vmem()] * 5,
        out_shape=[jax.ShapeDtypeStruct(weights.shape, jnp.bfloat16)]
        + [jax.ShapeDtypeStruct(asked.shape[2:], jnp.bfloat16)] * 4,
        scratch_shapes=query_scratch(asked) + update_scratch(pieces),
        compiler_params=pltpu.CompilerParams(vmem_limit_bytes=UPDATE_LIMIT),
        cost_estimate=SMALL,
        name="step",
    )(place, *pieces, asked, weights, target)
    return outs[1:]


def place_kernel(place, *refs):
    slabs, matrix, sems = refs[:8], refs[8], refs[9]
    part = slabs[0].shape[1]
    line, core, group = place[1], place[2], place[3]
    copies = []
    for idx, slab in enumerate(slabs):
        here_line = line ^ ((idx >> 1) & 1)
        here_group = group ^ (idx & 1)
        here_core = core ^ (idx >> 2)
        at = (here_line * 4 + here_group * 2 + here_core) * part
        rows = pl.ds(pl.multiple_of(at, part), part)
        copies.append(pltpu.make_async_copy(slab, matrix.at[:, rows], sems.at[idx]))
        copies[-1].start()
    for copy in copies:
        copy.wait()


def place_slabs(place, slabs):
    count, part, depth = slabs[0].shape
    return pl.pallas_call(
        place_kernel,
        in_specs=[smem()] + [hbm()] * 8,
        out_specs=vmem(),
        out_shape=jax.ShapeDtypeStruct((count, 8 * part, depth), jnp.bfloat16),
        scratch_shapes=[pltpu.SemaphoreType.DMA((8,))],
        compiler_params=pltpu.CompilerParams(vmem_limit_bytes=VMEM_LIMIT),
        cost_estimate=SMALL,
        name="place_slabs",
    )(place, *slabs)


def project_rows(row, out, mixed, matrix):
    total = None
    for turn in range(4):
        term = dot(mixed[turn][...], matrix[row ^ turn], 1, 0)
        total = term if total is None else total + term
    out[...] = total.astype(jnp.bfloat16)


def project_first(place, *refs):
    project_rows(place[0], refs[5], refs[:4], refs[4])


def project_second(place, *refs):
    mixed, first, matrix, out = refs[:4], refs[4], refs[5], refs[6]
    out[0] = first[...]
    project_rows(place[0], out.at[1], mixed, matrix)


def project(place, mixed, first, matrix):
    half = mixed[0].shape[0]
    depth = matrix.shape[2]
    shape = (half, depth) if first is None else (2, half, depth)
    args = (*mixed, matrix) if first is None else (*mixed, first, matrix)
    return pl.pallas_call(
        project_first if first is None else project_second,
        in_specs=[smem()] + [vmem()] * len(args),
        out_specs=vmem(),
        out_shape=jax.ShapeDtypeStruct(shape, jnp.bfloat16),
        compiler_params=pltpu.CompilerParams(vmem_limit_bytes=VMEM_LIMIT),
        cost_estimate=SMALL,
        name="project",
    )(place, *args)


def routes(rule):
    pairs = []
    for row in range(4):
        for line in range(2):
            for core in range(2):
                to_row, to_line, to_core = rule(row, line, core)
                pairs.append(((row * 2 + line) * 2 + core, (to_row * 2 + to_line) * 2 + to_core))
    return pairs


def swap_line(arr):
    return lax.ppermute(arr, BOTH, routes(lambda row, line, core: (row, 1 - line, core)))


def swap_core(arr):
    return lax.ppermute(arr, BOTH, routes(lambda row, line, core: (row, line, 1 - core)))


def swap_row(arr, turn):
    return lax.ppermute(arr, BOTH, routes(lambda row, line, core: (row ^ turn, line, core)))


def swap_group(arr):
    return lax.ppermute(arr, "groups", [(0, 1), (1, 0)])


def after(arr, *earlier):
    return lax.optimization_barrier((arr,) + earlier)[0]


def exchange(arr):
    groups = [[2 * row + line for row in range(4)] for line in range(2)]
    return lax.all_to_all(arr, "seq", 0, 0, axis_index_groups=groups, tiled=True)


def local_gathered(queries, keys, values, rates, fast_init, out_proj):
    seq, core, group = lax.axis_index("seq"), lax.axis_index("head"), lax.axis_index("groups")
    row, line = seq // 2, seq % 2
    place = jnp.stack([row, line, core, group]).astype(jnp.int32)
    rates = rates.transpose(0, 2, 1)

    part = out_proj.shape[0] // 4
    quarter = lax.dynamic_slice_in_dim(out_proj, (2 * group + core) * part, part, 0)
    quarters = jnp.broadcast_to(quarter[None], (4,) + quarter.shape)
    slab = exchange(quarters)
    kept, sent = pack(place, after(queries, quarters), keys, values, rates)
    dealt = deal(place, kept, swap_core(sent))
    swapped = swap_core(fast_init)

    own = exchange(after(dealt[0], swapped, slab))
    slab_line = swap_line(slab)
    slab_group = swap_group(slab)
    own_next = exchange(after(dealt[1], own))
    other = swap_line(after(own, slab_line, slab_group))
    own_core = swap_core(own)
    slab_both = swap_group(slab_line)
    asked = exchange(after(dealt[2], own_next, own_core, other))
    other_next = swap_line(own_next)
    own_next_core = swap_core(own_next)
    first, target = first_update(
        place, [own, own_core, other, swap_core(other)], fast_init, swapped
    )
    produced = apply(place, 0, asked, first)
    mixed = [[produced[0]] + [swap_row(produced[turn], turn) for turn in (1, 2, 3)]]
    other_next_core = swap_core(after(other_next, first))
    slabs = [slab, slab_group, slab_line, slab_both]
    slabs = slabs + [swap_core(after(arr, own_next)) for arr in slabs]
    pieces = [own_next, own_next_core, other_next, other_next_core]
    produced = step(place, 1, pieces, asked, after(first, *slabs[4:]), target)
    produced = [produced[0]] + [after(arr, *mixed[0][1:]) for arr in produced[1:]]
    mixed += [[produced[0]] + [swap_row(produced[turn], turn) for turn in (1, 2, 3)]]

    matrix = place_slabs(place, slabs)
    return project(place, mixed[1], project(place, mixed[0], None, matrix), matrix)


def solution(mesh):
    in_specs = (
        P(None, ("groups", "seq"), "head"),
        P(None, ("groups", "seq"), "head"),
        P(None, ("groups", "seq"), "head"),
        P(None, ("groups", "seq"), "head"),
        P(None, "head", None, None),
        P("seq", None),
    )
    out_specs = P(None, ("groups", "seq", "head"), None)
    few = dict(mesh.shape) == {"groups": 2, "seq": 8, "head": 2}
    local = local_gathered if few else local_summed
    return jax.shard_map(local, mesh=mesh, in_specs=in_specs, out_specs=out_specs, check_vma=False)
```

```python
import functools

import jax
import jax.numpy as jnp
from jax import lax
from jax.experimental import pallas as pl
from jax.experimental.pallas import tpu as pltpu
from jax.sharding import PartitionSpec as P

VMEM_LIMIT = 24 * 1024 * 1024
UPDATE_LIMIT = 45 * 1024 * 1024
BOTH = ("seq", "head")
SMALL = pl.CostEstimate(flops=1, bytes_accessed=1, transcendentals=0)


def silu_parts(value):
    sigma = jax.nn.sigmoid(value)
    return (value * sigma, sigma * (1.0 + value * (1.0 - sigma)))


def dot(left, right, left_dim, right_dim):
    return lax.dot_general(
        left, right, (((left_dim,), (right_dim,)), ((), ())), preferred_element_type=jnp.float32
    )


def local_update(weights, keys_local, values_local, rates_local):
    gate_pre = jnp.einsum(
        "thi,hoi->tho", keys_local, weights[0], preferred_element_type=jnp.float32
    )
    up_pre = jnp.einsum("thi,hoi->tho", keys_local, weights[1], preferred_element_type=jnp.float32)
    gate_act, gate_slope = silu_parts(gate_pre)
    hidden = (gate_act * up_pre).astype(jnp.bfloat16)
    weighted = (rates_local[:, :, None] * values_local.astype(jnp.float32)).astype(jnp.bfloat16)
    back = jnp.einsum("tho,hog->thg", weighted, weights[2], preferred_element_type=jnp.float32)
    grad_gate = (back * up_pre * gate_slope).astype(jnp.bfloat16)
    grad_up = (back * gate_act).astype(jnp.bfloat16)
    return jnp.stack(
        [
            jnp.einsum("thg,thi->hgi", grad_gate, keys_local, preferred_element_type=jnp.float32),
            jnp.einsum("thg,thi->hgi", grad_up, keys_local, preferred_element_type=jnp.float32),
            jnp.einsum("tho,thg->hog", weighted, hidden, preferred_element_type=jnp.float32),
        ]
    )


def apply_local(weights, queries_local):
    gate_pre = jnp.einsum(
        "thi,hoi->tho", queries_local, weights[0], preferred_element_type=jnp.float32
    )
    up_pre = jnp.einsum(
        "thi,hoi->tho", queries_local, weights[1], preferred_element_type=jnp.float32
    )
    gate_act, gate_slope = silu_parts(gate_pre)
    applied = (gate_act * up_pre).astype(jnp.bfloat16)
    produced = jnp.einsum("thg,hog->tho", applied, weights[2], preferred_element_type=jnp.float32)
    return produced.astype(jnp.bfloat16).reshape(queries_local.shape[0], -1)


def local_summed(queries, keys, values, rates, fast_init, out_proj):
    block_count, tok_count, width_here = queries.shape
    heads_here = fast_init.shape[1]
    head_width = fast_init.shape[2]
    init_float = fast_init.astype(jnp.float32)
    target = jnp.sqrt(jnp.mean(init_float * init_float, axis=-1, keepdims=True))
    row_count = head_width // lax.axis_size("seq")
    offset = lax.axis_index("seq") * row_count
    current = fast_init
    produced_list = []
    for block_idx in range(block_count):
        keys_local = keys[block_idx].reshape(tok_count, heads_here, head_width)
        values_local = values[block_idx].reshape(tok_count, heads_here, head_width)
        update = local_update(current, keys_local, values_local, rates[block_idx])
        shard = lax.psum_scatter(update, "seq", scatter_dimension=3, tiled=True)
        own = lax.dynamic_slice_in_dim(current, offset, row_count, 3).astype(jnp.float32) + shard
        squares = lax.psum(jnp.sum(own * own, axis=-1, keepdims=True), "seq")
        fresh = (own * target * lax.rsqrt(squares / head_width + 1e-06)).astype(jnp.bfloat16)
        current = lax.all_gather(fresh, "seq", axis=3, tiled=True)
        produced = apply_local(
            current, queries[block_idx].reshape(tok_count, heads_here, head_width)
        )
        produced_list.append(produced)
    mixed = lax.all_to_all(
        jnp.stack(produced_list), "head", split_axis=1, concat_axis=2, tiled=True
    )
    result = jnp.einsum(
        "ctf,fd->ctd",
        mixed,
        lax.all_gather(out_proj, "seq", axis=0, tiled=True),
        preferred_element_type=jnp.float32,
    )
    return result.astype(jnp.bfloat16)


def pack_kernel(place, queries, keys, values, rates, kept, sent, keys_in, values_in, queries_in, *sems):
    load_sems, out_sems = sems
    half = kept.shape[1]
    blocks = keys_in.shape[0]
    core = place[2]
    loads = []
    for block in range(blocks):
        for source, target in ((values, values_in), (keys, keys_in), (queries, queries_in)):
            sem = load_sems.at[len(loads)]
            loads.append(pltpu.make_async_copy(source.at[block], target.at[block], sem))
            loads[-1].start()
    copies = []

    def send(source, block, slot):
        for out, which in ((sent, 1 - core), (kept, core)):
            rows = pl.ds(pl.multiple_of(which * half, half), half)
            sem = out_sems.at[len(copies)]
            copies.append(pltpu.make_async_copy(source.at[block, rows], out.at[slot], sem))
            copies[-1].start()

    for block in range(blocks):
        for load in loads[3 * block : 3 * block + 3]:
            load.wait()
        send(keys_in, block, 2 * block)
        send(queries_in, block, 2 * blocks + block)
        rate = rates[block].T
        width = keys_in.shape[2] // 2
        for head in range(2):
            cols = slice(head * width, (head + 1) * width)
            scaled = rate[:, head : head + 1] * values_in[block, :, cols].astype(jnp.float32)
            values_in[block, :, cols] = scaled.astype(jnp.bfloat16)
        send(values_in, block, 2 * block + 1)
    for copy in copies:
        copy.wait()


def pack(place, queries, keys, values, rates):
    blocks, tokens, both = keys.shape
    out = jax.ShapeDtypeStruct((3 * blocks, tokens // 2, both), jnp.bfloat16)
    return pl.pallas_call(
        pack_kernel,
        in_specs=[smem(), hbm(), hbm(), hbm(), vmem()],
        out_specs=[pl.BlockSpec(memory_space=pl.ANY)] * 2,
        out_shape=[out, out],
        scratch_shapes=[pltpu.VMEM(keys.shape, jnp.bfloat16)] * 3
        + [pltpu.SemaphoreType.DMA((3 * blocks,)), pltpu.SemaphoreType.DMA((6 * blocks,))],
        cost_estimate=SMALL,
        name="pack",
    )(place, queries, keys, values, rates)


def deal_kernel(place, kept, got, *refs):
    outs, (held, load_sems, sems) = refs[:-3], refs[-3:]
    width = outs[0].shape[3]
    core = place[2]
    loads = [
        pltpu.make_async_copy(kept, held.at[core], load_sems.at[0]),
        pltpu.make_async_copy(got, held.at[1 - core], load_sems.at[1]),
    ]
    for load in loads:
        load.start()
    for load in loads:
        load.wait()
    copies = []
    for idx, out in enumerate(outs):
        for head in range(4):
            source = held.at[head // 2, pl.ds(2 * idx, 2), :, pl.ds((head % 2) * width, width)]
            copies.append(pltpu.make_async_copy(source, out.at[head], sems.at[len(copies)]))
            copies[-1].start()
    for copy in copies:
        copy.wait()


def deal(place, kept, got):
    kinds, half, both = kept.shape
    out = jax.ShapeDtypeStruct((4, 2, half, both // 2), jnp.bfloat16)
    return pl.pallas_call(
        deal_kernel,
        in_specs=[smem(), hbm(), hbm()],
        out_specs=[pl.BlockSpec(memory_space=pl.ANY)] * (kinds // 2),
        out_shape=[out] * (kinds // 2),
        scratch_shapes=[
            pltpu.VMEM((2,) + kept.shape, jnp.bfloat16),
            pltpu.SemaphoreType.DMA((2,)),
            pltpu.SemaphoreType.DMA((2 * kinds,)),
        ],
        cost_estimate=SMALL,
        name="deal",
    )(place, kept, got)


def start_pieces(pieces, scratch):
    keys, values, sems = scratch[0], scratch[1], scratch[5]
    count, half = pieces[0].shape[0], pieces[0].shape[2]
    copies = []
    for idx, piece in enumerate(pieces):
        for source in range(count):
            rows = pl.ds((count * idx + source) * half, half)
            for kind, buf in enumerate((keys, values)):
                sem = sems.at[len(copies)]
                copies.append(pltpu.make_async_copy(piece.at[source, kind], buf.at[rows], sem))
                copies[-1].start()
    return copies


def form_update(copies, count, weights, target, fresh, scratch):
    keys, values, hidden, grad_gate, grad_up, _ = scratch
    tile, share = keys.shape[0] // count, len(copies) // count
    for idx in range(count):
        for copy in copies[share * idx : share * (idx + 1)]:
            copy.wait()
        rows = pl.ds(idx * tile, tile)
        key, value = keys[rows], values[rows]
        gate_pre = dot(key, weights[0], 1, 1)
        up_pre = dot(key, weights[1], 1, 1)
        back = dot(value, weights[2], 1, 0)
        gate_act, gate_slope = silu_parts(gate_pre)
        hidden[rows] = (gate_act * up_pre).astype(jnp.bfloat16)
        grad_gate[rows] = (back * up_pre * gate_slope).astype(jnp.bfloat16)
        grad_up[rows] = (back * gate_act).astype(jnp.bfloat16)
    for idx, (left, right) in enumerate(((grad_gate, keys), (grad_up, keys), (values, hidden))):
        summed = weights[idx].astype(jnp.float32) + dot(left[...], right[...], 0, 0)
        mean = jnp.mean(summed * summed, axis=-1, keepdims=True)
        fresh[idx] = (summed * target[idx] * lax.rsqrt(mean + 1e-06)).astype(jnp.bfloat16)


def start_queries(block, place, asked, queries, sems):
    half = asked.shape[2]
    row = place[0]
    copies = []
    for source in range(asked.shape[0]):
        rows = pl.ds(pl.multiple_of((row ^ source) * half, half), half)
        copies.append(
            pltpu.make_async_copy(asked.at[source, block], queries.at[rows], sems.at[source])
        )
        copies[-1].start()
    return copies


def form_outputs(query, weights, produced):
    half = produced[0].shape[0]
    gate_pre = dot(query, weights[0], 1, 1)
    up_pre = dot(query, weights[1], 1, 1)
    applied = (gate_pre * jax.nn.sigmoid(gate_pre) * up_pre).astype(jnp.bfloat16)
    out = dot(applied, weights[2], 1, 1).astype(jnp.bfloat16)
    for idx, ref in enumerate(produced):
        ref[...] = out[idx * half : (idx + 1) * half]


def step_kernel(block, place, *refs):
    pieces, asked, weights, target, fresh = refs[:4], refs[4], refs[5], refs[6], refs[7]
    produced, (queries, query_sems) = refs[8:12], refs[12:14]
    copies = start_queries(block, place, asked, queries, query_sems)
    form_update(start_pieces(pieces, refs[14:]), 2, weights, target, fresh, refs[14:])
    for copy in copies:
        copy.wait()
    form_outputs(queries[...], fresh, produced)


def first_kernel(place, *refs):
    pieces = refs[:4]
    held, swapped, fresh, target, weights, sem = refs[4:10]
    row, core = place[0], place[2]

    def load(source):
        copy = pltpu.make_async_copy(source.at[:, row % 2], weights, sem.at[0])
        copy.start()
        copy.wait()

    copies = start_pieces(pieces, refs[10:])

    @pl.when(core == row // 2)
    def _():
        load(held)

    @pl.when(core != row // 2)
    def _():
        load(swapped)

    for idx in range(weights.shape[0]):
        init = weights[idx].astype(jnp.float32)
        target[idx] = jnp.sqrt(jnp.mean(init * init, axis=-1, keepdims=True))
    form_update(copies, 2, weights, target, fresh, refs[10:])


def apply_kernel(block, place, *refs):
    asked, weights, produced, queries, sems = refs[0], refs[1], refs[2:6], refs[6], refs[7]
    for copy in start_queries(block, place, asked, queries, sems):
        copy.wait()
    form_outputs(queries[...], weights, produced)


def vmem():
    return pl.BlockSpec(memory_space=pltpu.VMEM)


def hbm():
    return pl.BlockSpec(memory_space=pl.ANY)


def smem():
    return pl.BlockSpec(memory_space=pltpu.SMEM)


def update_scratch(pieces):
    count, _, half, width = pieces[0].shape
    buf = pltpu.VMEM((count * len(pieces) * half, width), jnp.bfloat16)
    return [buf] * 5 + [pltpu.SemaphoreType.DMA((2 * count * len(pieces),))]


def query_scratch(asked):
    count, _, half, width = asked.shape
    return [
        pltpu.VMEM((count * half, width), jnp.bfloat16),
        pltpu.SemaphoreType.DMA((count,)),
    ]


def first_update(place, pieces, held, swapped):
    kinds, _, rows, cols = held.shape
    return pl.pallas_call(
        first_kernel,
        in_specs=[smem()] + [hbm()] * 6,
        out_specs=[vmem(), vmem()],
        out_shape=[
            jax.ShapeDtypeStruct((kinds, rows, cols), jnp.bfloat16),
            jax.ShapeDtypeStruct((kinds, rows, 1), jnp.float32),
        ],
        scratch_shapes=[
            pltpu.VMEM((kinds, rows, cols), jnp.bfloat16),
            pltpu.SemaphoreType.DMA((1,)),
        ]
        + update_scratch(pieces),
        compiler_params=pltpu.CompilerParams(vmem_limit_bytes=UPDATE_LIMIT),
        cost_estimate=SMALL,
        name="first_update",
    )(place, *pieces, held, swapped)


def apply(place, block, asked, weights):
    return pl.pallas_call(
        functools.partial(apply_kernel, block),
        in_specs=[smem(), hbm(), vmem()],
        out_specs=[vmem()] * 4,
        out_shape=[jax.ShapeDtypeStruct(asked.shape[2:], jnp.bfloat16)] * 4,
        scratch_shapes=query_scratch(asked),
        compiler_params=pltpu.CompilerParams(vmem_limit_bytes=VMEM_LIMIT),
        cost_estimate=SMALL,
        name="apply",
    )(place, asked, weights)


def step(place, block, pieces, asked, weights, target):
    outs = pl.pallas_call(
        functools.partial(step_kernel, block),
        in_specs=[smem()] + [hbm()] * 5 + [vmem(), vmem()],
        out_specs=[vmem()] * 5,
        out_shape=[jax.ShapeDtypeStruct(weights.shape, jnp.bfloat16)]
        + [jax.ShapeDtypeStruct(asked.shape[2:], jnp.bfloat16)] * 4,
        scratch_shapes=query_scratch(asked) + update_scratch(pieces),
        compiler_params=pltpu.CompilerParams(vmem_limit_bytes=UPDATE_LIMIT),
        cost_estimate=SMALL,
        name="step",
    )(place, *pieces, asked, weights, target)
    return outs[1:]


def place_kernel(place, *refs):
    slabs, matrix, sems = refs[:8], refs[8], refs[9]
    part = slabs[0].shape[1]
    line, core, group = place[1], place[2], place[3]
    copies = []
    for idx, slab in enumerate(slabs):
        here_line = line ^ ((idx >> 1) & 1)
        here_group = group ^ (idx & 1)
        here_core = core ^ (idx >> 2)
        at = (here_line * 4 + here_group * 2 + here_core) * part
        rows = pl.ds(pl.multiple_of(at, part), part)
        copies.append(pltpu.make_async_copy(slab, matrix.at[:, rows], sems.at[idx]))
        copies[-1].start()
    for copy in copies:
        copy.wait()


def place_slabs(place, slabs):
    count, part, depth = slabs[0].shape
    return pl.pallas_call(
        place_kernel,
        in_specs=[smem()] + [hbm()] * 8,
        out_specs=vmem(),
        out_shape=jax.ShapeDtypeStruct((count, 8 * part, depth), jnp.bfloat16),
        scratch_shapes=[pltpu.SemaphoreType.DMA((8,))],
        compiler_params=pltpu.CompilerParams(vmem_limit_bytes=VMEM_LIMIT),
        cost_estimate=SMALL,
        name="place_slabs",
    )(place, *slabs)


def project_rows(row, out, mixed, matrix):
    total = None
    for turn in range(4):
        term = dot(mixed[turn][...], matrix[row ^ turn], 1, 0)
        total = term if total is None else total + term
    out[...] = total.astype(jnp.bfloat16)


def project_first(place, *refs):
    project_rows(place[0], refs[5], refs[:4], refs[4])


def project_second(place, *refs):
    mixed, first, matrix, out = refs[:4], refs[4], refs[5], refs[6]
    out[0] = first[...]
    project_rows(place[0], out.at[1], mixed, matrix)


def project(place, mixed, first, matrix):
    half = mixed[0].shape[0]
    depth = matrix.shape[2]
    shape = (half, depth) if first is None else (2, half, depth)
    args = (*mixed, matrix) if first is None else (*mixed, first, matrix)
    return pl.pallas_call(
        project_first if first is None else project_second,
        in_specs=[smem()] + [vmem()] * len(args),
        out_specs=vmem(),
        out_shape=jax.ShapeDtypeStruct(shape, jnp.bfloat16),
        compiler_params=pltpu.CompilerParams(vmem_limit_bytes=VMEM_LIMIT),
        cost_estimate=SMALL,
        name="project",
    )(place, *args)


def routes(rule):
    pairs = []
    for row in range(4):
        for line in range(2):
            for core in range(2):
                to_row, to_line, to_core = rule(row, line, core)
                pairs.append(((row * 2 + line) * 2 + core, (to_row * 2 + to_line) * 2 + to_core))
    return pairs


def swap_line(arr):
    return lax.ppermute(arr, BOTH, routes(lambda row, line, core: (row, 1 - line, core)))


def swap_core(arr):
    return lax.ppermute(arr, BOTH, routes(lambda row, line, core: (row, line, 1 - core)))


def swap_row(arr, turn):
    return lax.ppermute(arr, BOTH, routes(lambda row, line, core: (row ^ turn, line, core)))


def swap_group(arr):
    return lax.ppermute(arr, "groups", [(0, 1), (1, 0)])


def after(arr, *earlier):
    return lax.optimization_barrier((arr,) + earlier)[0]


def exchange(arr):
    groups = [[2 * row + line for row in range(4)] for line in range(2)]
    return lax.all_to_all(arr, "seq", 0, 0, axis_index_groups=groups, tiled=True)


def local_gathered(queries, keys, values, rates, fast_init, out_proj):
    seq, core, group = lax.axis_index("seq"), lax.axis_index("head"), lax.axis_index("groups")
    row, line = seq // 2, seq % 2
    place = jnp.stack([row, line, core, group]).astype(jnp.int32)
    rates = rates.transpose(0, 2, 1)

    part = out_proj.shape[0] // 4
    quarter = lax.dynamic_slice_in_dim(out_proj, (2 * group + core) * part, part, 0)
    quarters = jnp.broadcast_to(quarter[None], (4,) + quarter.shape)
    slab = exchange(quarters)
    kept, sent = pack(place, after(queries, quarters), keys, values, rates)
    dealt = deal(place, kept, swap_core(sent))
    swapped = swap_core(fast_init)

    own = exchange(after(dealt[0], swapped, slab))
    slab_line = swap_line(slab)
    slab_group = swap_group(slab)
    own_next = exchange(after(dealt[1], own))
    other = swap_line(after(own, slab_line, slab_group))
    own_core = swap_core(own)
    slab_both = swap_group(slab_line)
    asked = exchange(after(dealt[2], own_next, own_core, other))
    other_next = swap_line(own_next)
    own_next_core = swap_core(own_next)
    first, target = first_update(
        place, [own, own_core, other, swap_core(other)], fast_init, swapped
    )
    produced = apply(place, 0, asked, first)
    mixed = [[produced[0]] + [swap_row(produced[turn], turn) for turn in (1, 2, 3)]]
    other_next_core = swap_core(after(other_next, first))
    slabs = [slab, slab_group, slab_line, slab_both]
    slabs = slabs + [swap_core(after(arr, own_next)) for arr in slabs]
    pieces = [own_next, own_next_core, other_next, other_next_core]
    produced = step(place, 1, pieces, asked, after(first, *slabs[4:]), target)
    produced = [produced[0]] + [after(arr, *mixed[0][1:]) for arr in produced[1:]]
    mixed += [[produced[0]] + [swap_row(produced[turn], turn) for turn in (1, 2, 3)]]

    matrix = place_slabs(place, slabs)
    return project(place, mixed[1], project(place, mixed[0], None, matrix), matrix)


def solution(mesh):
    in_specs = (
        P(None, ("groups", "seq"), "head"),
        P(None, ("groups", "seq"), "head"),
        P(None, ("groups", "seq"), "head"),
        P(None, ("groups", "seq"), "head"),
        P(None, "head", None, None),
        P("seq", None),
    )
    out_specs = P(None, ("groups", "seq", "head"), None)
    few = dict(mesh.shape) == {"groups": 2, "seq": 8, "head": 2}
    local = local_gathered if few else local_summed
    return jax.shard_map(local, mesh=mesh, in_specs=in_specs, out_specs=out_specs, check_vma=False)
```
